1024 devices in a mesh: dp: 128 (over y, x, core), tensor: 8 (over z).
Axes of the slice: x: 8, y: 8, z: 8, core: 2. Of those that a mesh axis runs over, the one named last changes fastest.
Arguments:
- gradient: bfloat16 [128, 512, 512], P(None, 'dp', 'tensor')
- left_root: float32 [256, 512, 512], P('dp')
- right_root: float32 [256, 512, 512], P('dp')
- counts: int32 [128], replicated, may hold values from 0 to 2, as said below
- slot_table: int32 [128, 2], replicated, may hold values from 0 to 127
Outputs:
- update: bfloat16 [128, 512, 512], P(None, 'dp', 'tensor')
The draws below stay inside these ranges and needn't reach their ends.
Inputs may be any that keep to these rules, and one draw needn't show every extreme that they name: Owner o holds the blocks slot_table[o, 0] to slot_table[o, counts[o] - 1]; over all owners every block is held exactly once; the other entries of slot_table are arbitrary block numbers.
All inputs are finite; a program needn't handle non-finite values.
Results may differ from the reference program's by a relative error of at most 0.001.
Values may be sent and summed in bfloat16 or wider, within the bound.
A program may use at most 32 MiB of HBM per device.

```python
import math
import jax
import jax.numpy as jnp
from jax import lax

BLK = 512
CAP = 2
NB = 128
N_DP = 128


def owner_plan(key):
    first_key, second_key, third_key = jax.random.split(key, 3)
    places = jnp.arange(N_DP, dtype=jnp.int32)
    pattern = jnp.where(places < N_DP // 4, 2, jnp.where(places < 3 * N_DP // 4, 1, 0)).astype(jnp.int32)
    owner_counts = pattern[jax.random.permutation(first_key, N_DP)]
    living = (jnp.arange(CAP, dtype=jnp.int32)[None, :] < owner_counts[:, None]).reshape(-1)
    ranks = jnp.clip(jnp.cumsum(living.astype(jnp.int32)) - 1, 0, NB - 1)
    shuffled = jax.random.permutation(second_key, NB).astype(jnp.int32)
    filler = jax.random.randint(third_key, (N_DP * CAP,), 0, NB).astype(jnp.int32)
    table = jnp.where(living, shuffled[ranks], filler).reshape(N_DP, CAP)
    return (owner_counts.astype(jnp.int32), table.astype(jnp.int32))


def root_factor(key, spread):
    diag_key, noise_key = jax.random.split(key)
    diagonal = jnp.exp(jax.random.uniform(diag_key, (N_DP * CAP, BLK), jnp.float32, math.log(0.5), math.log(2.0)))
    noise = jax.random.normal(noise_key, (N_DP * CAP, BLK, BLK), jnp.float32) * (spread / math.sqrt(BLK))
    symmetric = (noise + jnp.swapaxes(noise, 1, 2)) * 0.7071
    return (symmetric + diagonal[:, :, None] * jnp.eye(BLK, dtype=jnp.float32)[None, :, :]).astype(jnp.float32)


def draw_counts(key, part):
    return owner_plan(key)[0]


def draw_slot_table(key, part):
    return owner_plan(key)[1]


def draw_left_root(key, part):
    key = jax.random.fold_in(key, 21)
    return root_factor(key, 0.5)


def draw_right_root(key, part):
    key = jax.random.fold_in(key, 37)
    return root_factor(key, 0.5)


def draw_gradient(key, part):
    key = jax.random.fold_in(key, 11)
    base_key, row_key, col_key = jax.random.split(key, 3)
    shape = (NB, BLK, BLK)
    spread = math.log(4.0)
    base = jnp.clip(jax.random.normal(base_key, shape, jnp.float32), -4.0, 4.0)
    row_scale = jnp.exp(jax.random.uniform(row_key, (NB, BLK, 1), jnp.float32, 0.0, spread))
    col_scale = jnp.exp(jax.random.uniform(col_key, (NB, 1, BLK), jnp.float32, 0.0, spread))
    return (0.3 * base * row_scale * col_scale).astype(jnp.bfloat16)


def setup_inputs(seed: int = 0) -> dict:
    key_list = jax.random.split(jax.random.key(seed), 6)
    gradient = draw_gradient(jax.random.fold_in(key_list[5], 71), 0)
    left_root = draw_left_root(jax.random.fold_in(key_list[5], 71), 0)
    right_root = draw_right_root(jax.random.fold_in(key_list[5], 71), 0)
    counts = draw_counts(jax.random.fold_in(key_list[5], 71), 0)
    slot_table = draw_slot_table(jax.random.fold_in(key_list[5], 71), 0)
    return dict(gradient=gradient, left_root=left_root, right_root=right_root, counts=counts, slot_table=slot_table)


EPSILON = 1e-06
HIGHEST_PRECISION = lax.Precision.HIGHEST

def reference(gradient, left_root, right_root, counts, slot_table):
    block_ids = slot_table.reshape(-1).astype(jnp.int32)
    living = (jnp.arange(CAP, dtype=jnp.int32)[None, :] < counts[:, None]).reshape(-1)

    def one_slot(index):
        block = gradient[block_ids[index]].astype(jnp.float32)
        middle = jnp.dot(block, right_root[index], precision=HIGHEST_PRECISION, preferred_element_type=jnp.float32)
        direction = jnp.dot(left_root[index], middle, precision=HIGHEST_PRECISION, preferred_element_type=jnp.float32)
        grad_mean = jnp.mean(block * block)
        dir_mean = jnp.mean(direction * direction)
        factor = jnp.sqrt(grad_mean) * lax.rsqrt(dir_mean + EPSILON)
        return (direction * factor).astype(jnp.bfloat16)
    results = lax.map(one_slot, jnp.arange(N_DP * CAP, dtype=jnp.int32))
    targets = jnp.where(living, block_ids, NB).astype(jnp.int32)
    holder = jnp.zeros((NB + 1, BLK, BLK), jnp.bfloat16).at[targets].set(results)
    return holder[:NB]
```

```python
import jax
import jax.numpy as jnp
from jax import lax
from jax.experimental import pallas as pl
from jax.experimental.pallas import tpu as pltpu
from jax.sharding import PartitionSpec as P

MESH = pl.DeviceIdType.MESH
EPSILON = 1e-06
BLK = 512
NB = 128
NY, NX, NXC, NZ = 8, 8, 16, 8
F32, BF16 = jnp.float32, jnp.bfloat16
FAR_FIRST = (4, 3, 5, 2, 6, 1, 7, 0)


def ring_distance(step):
    return min(step, 8 - step)


YZ_STEPS = sorted(
    ((dy, dz) for dy in range(8) for dz in range(8)),
    key=lambda s: -(ring_distance(s[0]) + ring_distance(s[1])),
)


def iota(shape, dim):
    return lax.broadcasted_iota(jnp.int32, shape, dim)


def one_where(mask):
    return jnp.where(mask, 1.0, 0.0).astype(BF16)


def dot(a, b):
    return jnp.dot(a, b, preferred_element_type=F32)


def dot_nt(a, b):
    return lax.dot_general(a, b, (((1,), (1,)), ((), ())), preferred_element_type=F32)


def dot_tn(a, b):
    return lax.dot_general(a, b, (((0,), (0,)), ((), ())), preferred_element_type=F32)


def split(value):
    high = value.astype(BF16)
    return high, (value - high.astype(F32)).astype(BF16)


def kernel(
    grad, left, right, counts, table, out,
    grad_v, left_v, right_v, counts_v, table_v,
    send1, recv1, send2, recv2, send3, recv3, send4, recv4,
    left_high, left_low, right_high, right_low, regroup, ungroup, place,
    local_sem, send_sem, recv_sem, group_sem,
):
    dp, z = lax.axis_index("dp"), lax.axis_index("tensor")
    y, xc = dp // NXC, lax.rem(dp, NXC)
    x, core = xc // 2, lax.rem(xc, 2)
    slot = z // 4
    is_handler = lax.rem(z, 4) == 2 * core + lax.rem(y, 2)

    def at_xc(dx, dc):
        return lax.rem(x + dx, NX) * 2 + lax.rem(core + dc, 2)

    xc_steps = [(dx, dc) for dx in FAR_FIRST for dc in (0, 1) if (dx, dc) != (0, 0)]

    barrier = pltpu.get_barrier_semaphore()
    peers = [{"dp": y * NXC + at_xc(dx, dc)} for dx, dc in xc_steps]
    peers += [{"dp": lax.rem(y + d, NY) * NXC + xc} for d in FAR_FIRST[:7]]
    peers += [{"tensor": lax.rem(z + d, NZ)} for d in FAR_FIRST[:7]]
    for peer in peers:
        pl.semaphore_signal(barrier, inc=1, device_id=peer, device_id_type=MESH)

    fetch = [
        pltpu.make_async_copy(table, table_v, local_sem.at[0]),
        pltpu.make_async_copy(counts, counts_v, local_sem.at[1]),
        pltpu.make_async_copy(grad, grad_v, local_sem.at[2]),
    ]
    for copy in fetch:
        copy.start()
    fetch_left = pltpu.make_async_copy(left.at[slot], left_v, local_sem.at[3])
    fetch_right = pltpu.make_async_copy(right.at[slot], right_v, local_sem.at[4])

    @pl.when(is_handler)
    def _():
        fetch_right.start()
        fetch_left.start()

    fetch[0].wait()
    fetch[1].wait()
    block = iota((NB, NB), 0)
    row, col = iota((256, 256), 0), iota((256, 256), 1)
    source = (row % 2) * 128 + ((row // 2) % 8) * 16 + row // 16
    order = one_where(col == source)
    hit = [block == table_v[c : c + 1, :] for c in (0, 1)]
    pick = dot_nt(order, one_where(jnp.concatenate(hit, axis=1))).astype(BF16)
    fetch[2].wait()
    for h in (0, 1):
        pieces = dot_nt(pick, grad_v[128 * h : 128 * h + 128, :]).astype(BF16)
        send1[:, 16 * h : 16 * h + 16, :] = pieces.reshape(NXC, 16, 128)

    pl.semaphore_wait(barrier, len(peers))
    for d in FAR_FIRST[:7]:
        pl.semaphore_signal(
            group_sem, inc=1, device_id={"dp": lax.rem(y + d, NY) * NXC + xc}, device_id_type=MESH
        )

    def put(source, target, phase, device):
        pltpu.make_async_remote_copy(
            src_ref=source,
            dst_ref=target,
            send_sem=send_sem.at[phase],
            recv_sem=recv_sem.at[phase],
            device_id=device,
            device_id_type=MESH,
        ).start()

    def put_here(source, target, phase):
        pltpu.make_async_copy(source, target, recv_sem.at[phase]).start()

    def arrived(ref, phase):
        pltpu.make_async_copy(ref, ref, recv_sem.at[phase]).wait()

    def sent(ref, phase):
        pltpu.make_async_copy(ref, ref, send_sem.at[phase]).wait()

    for dx, dc in xc_steps:
        there = at_xc(dx, dc)
        put(send1.at[there], recv1.at[xc], 0, {"dp": y * NXC + there})
    put_here(send1.at[xc], recv1.at[xc], 0)

    live = [hit[c] & (counts_v[0:1, :] > c) for c in (0, 1)]
    place[...] = dot_nt(order, one_where(jnp.concatenate(live, axis=1))).astype(BF16)
    row, col = iota((BLK, BLK), 0), iota((BLK, BLK), 1)
    regroup[...] = one_where(col == ((row // 2) % 16) * 32 + (row % 2) * 16 + row // 32)
    ungroup[...] = one_where(col == (row % 16) * 32 + (row // 32) * 2 + (row // 16) % 2)

    @pl.when(is_handler)
    def _():
        fetch_right.wait()
        high, low = split(right_v[...])
        right_high[...] = high
        right_low[...] = low
        fetch_left.wait()
        rows = one_where(col == (row % 256) * 2 + row // 256)
        columns = one_where(row == (col % 256) * 2 + col // 256)
        high, low = split(left_v[...])
        left_high[...] = dot(dot(rows, high).astype(BF16), columns).astype(BF16)
        left_low[...] = dot(dot(rows, low).astype(BF16), columns).astype(BF16)

    arrived(recv1, 0)
    grouped = dot(regroup[...], recv1[...].reshape(BLK, 128)).astype(BF16)
    send2[...] = grouped.reshape(16, 32, 128)

    pl.semaphore_wait(group_sem, 7)
    for dy in FAR_FIRST:
        there = lax.rem(y + dy, NY)
        for c in (0, 1):
            there_z = 4 * c + 2 * core + lax.rem(there, 2)
            source, target = send2.at[there * 2 + c], recv2.at[y, z]
            if dy:
                put(source, target, 1, {"dp": there * NXC + xc, "tensor": there_z})
                continue

            @pl.when(there_z != z)
            def _(source=source, target=target, there_z=there_z):
                put(source, target, 1, {"dp": dp, "tensor": there_z})

            @pl.when(there_z == z)
            def _(source=source, target=target):
                put_here(source, target, 1)

    @pl.when(is_handler)
    def _():
        arrived(recv2, 1)
        panels = [recv2[:, t].reshape(256, 128) for t in range(NZ)]
        even = [jnp.concatenate([panels[t][:, :64], panels[t + 1][:, :64]], axis=1) for t in range(0, NZ, 2)]
        odd = [jnp.concatenate([panels[t][:, 64:], panels[t + 1][:, 64:]], axis=1) for t in range(0, NZ, 2)]
        held = jnp.concatenate([jnp.concatenate(even, axis=1), jnp.concatenate(odd, axis=1)], axis=0)
        middle = dot(held, right_high[...]) + dot(held, right_low[...])
        high, low = split(middle)
        direction = dot(left_high[...], high) + dot(left_high[...], low) + dot(left_low[...], high)
        wide = held.astype(F32)
        entries = BLK * BLK
        grad_mean = jnp.sum(wide * wide, keepdims=True) / entries
        dir_mean = jnp.sum(direction * direction, keepdims=True) / entries
        factor = jnp.sqrt(grad_mean) * lax.rsqrt(dir_mean + EPSILON)
        mine = (iota((1, NB), 1) == dp) & (counts_v[...] > slot)
        alive = jnp.max(jnp.where(mine, 1.0, 0.0), keepdims=True) > 0.0
        update = jnp.where(alive, direction * factor, 0.0).astype(BF16)
        for t in range(0, NZ, 2):
            upper, lower = update[:256, 64 * t : 64 * t + 128], update[256:, 64 * t : 64 * t + 128]
            first = jnp.concatenate([upper[:, :64], lower[:, :64]], axis=1)
            second = jnp.concatenate([upper[:, 64:], lower[:, 64:]], axis=1)
            send3[:, t] = first.reshape(NY, 32, 128)
            send3[:, t + 1] = second.reshape(NY, 32, 128)
        for dy, dz in YZ_STEPS:
            there, there_z = lax.rem(y + dy, NY), lax.rem(z + dz, NZ)
            source, target = send3.at[there, there_z], recv3.at[y * 2 + slot]
            if dy or dz:
                put(source, target, 2, {"dp": there * NXC + xc, "tensor": there_z})
            else:
                put_here(source, target, 2)

    arrived(recv3, 2)
    grouped = dot(ungroup[...], recv3[...].reshape(BLK, 128)).astype(BF16)
    send4[...] = grouped.reshape(NXC, 32, 128)

    for dx, dc in xc_steps:
        there = at_xc(dx, dc)
        put(send4.at[there], recv4.at[xc], 3, {"dp": y * NXC + there})
    put_here(send4.at[xc], recv4.at[xc], 3)
    arrived(recv4, 3)
    for h in (0, 1):
        returned = recv4[:, 16 * h : 16 * h + 16, :].reshape(256, 128)
        out[128 * h : 128 * h + 128, :] = dot_tn(returned, place[...]).astype(BF16)

    sent(send1.at[pl.ds(0, 15)], 0)
    sent(send4.at[pl.ds(0, 15)], 3)

    @pl.when(is_handler)
    def _():
        sent(send2.at[pl.ds(0, 15)], 1)
        sent(send3.at[pl.ds(0, 7)], 2)
        sent(send3.at[0, pl.ds(0, 7)], 2)

    @pl.when(jnp.logical_not(is_handler))
    def _():
        sent(send2, 1)


def body(gradient, left_root, right_root, counts, slot_table):
    pieces = jnp.transpose(gradient, (1, 2, 0)).reshape(256, NB)
    vmem = pltpu.VMEM
    message = (32, 128)
    update = pl.pallas_call(
        kernel,
        out_shape=jax.ShapeDtypeStruct((256, NB), BF16),
        in_specs=[pl.BlockSpec(memory_space=pltpu.HBM)] * 5,
        out_specs=pl.BlockSpec(memory_space=pltpu.VMEM),
        scratch_shapes=[
            vmem((256, NB), BF16),
            vmem((BLK, BLK), F32),
            vmem((BLK, BLK), F32),
            vmem((1, NB), jnp.int32),
            vmem((2, NB), jnp.int32),
            vmem((16, *message), BF16),
            vmem((16, *message), BF16),
            vmem((16, *message), BF16),
            vmem((NY, NZ, *message), BF16),
            vmem((NY, NZ, *message), BF16),
            vmem((16, *message), BF16),
            vmem((16, *message), BF16),
            vmem((16, *message), BF16),
            vmem((BLK, BLK), BF16),
            vmem((BLK, BLK), BF16),
            vmem((BLK, BLK), BF16),
            vmem((BLK, BLK), BF16),
            vmem((BLK, BLK), BF16),
            vmem((BLK, BLK), BF16),
            vmem((256, NB), BF16),
            pltpu.SemaphoreType.DMA((5,)),
            pltpu.SemaphoreType.DMA((4,)),
            pltpu.SemaphoreType.DMA((4,)),
            pltpu.SemaphoreType.REGULAR,
        ],
        compiler_params=pltpu.CompilerParams(
            collective_id=0, has_side_effects=True, vmem_limit_bytes=63 * 1024 * 1024
        ),
    )(pieces, left_root, right_root, counts.reshape(1, NB), slot_table.T)
    return jnp.transpose(update.reshape(4, 64, NB), (2, 0, 1))


def solution(mesh):
    return jax.shard_map(
        body,
        mesh=mesh,
        in_specs=(P(None, "dp", "tensor"), P("dp", None, None), P("dp", None, None), P(), P()),
        out_specs=P(None, "dp", "tensor"),
        check_vma=False,
    )
```

```python
import jax
import jax.numpy as jnp
from jax import lax
from jax.experimental import pallas as pl
from jax.experimental.pallas import tpu as pltpu
from jax.sharding import PartitionSpec as P

MESH = pl.DeviceIdType.MESH
EPSILON = 1e-06
BLK = 512
NB = 128
NY, NX, NXC, NZ = 8, 8, 16, 8
F32, BF16 = jnp.float32, jnp.bfloat16
PLANES = 4
FAR_FIRST = (4, 3, 5, 2, 6, 1, 7, 0)
EARLY_X = (0, 1, 2, 7, 3, 6, 5, 4)
EARLY_Y = (0, 1, 2, 3, 7, 6, 5, 4)


def iota(shape, dim):
    return lax.broadcasted_iota(jnp.int32, shape, dim)


def one_where(mask):
    return jnp.where(mask, 1.0, 0.0).astype(BF16)


def dot(a, b):
    return jnp.dot(a, b, preferred_element_type=F32)


def dot_nt(a, b):
    return lax.dot_general(a, b, (((1,), (1,)), ((), ())), preferred_element_type=F32)


def dot_tn(a, b):
    return lax.dot_general(a, b, (((0,), (0,)), ((), ())), preferred_element_type=F32)


def split(value):
    high = value.astype(BF16)
    return high, (value - high.astype(F32)).astype(BF16)


def kernel(
    grad, left, right, counts, table, out,
    grad_v, left_v, right_v, counts_v, table_v,
    send1, recv1, send2, recv2, send3, recv3, send4, recv4,
    left_high, left_low, right_high, right_low, ungroup, place, partial,
    local_sem, send_sem, recv_sem, piece_sem, panel_sem,
):
    dp, z = lax.axis_index("dp"), lax.axis_index("tensor")
    y, xc = dp // NXC, lax.rem(dp, NXC)
    x, core = xc // 2, lax.rem(xc, 2)
    slot = lax.rem(z // 2, 2)
    relays = z < PLANES
    handles = relays & (core == lax.rem(z, 2))

    fetch = [
        pltpu.make_async_copy(table, table_v, local_sem.at[0]),
        pltpu.make_async_copy(grad, grad_v, local_sem.at[1]),
        pltpu.make_async_copy(counts, counts_v, local_sem.at[2]),
    ]
    for copy in fetch:
        copy.start()
    fetch_left = pltpu.make_async_copy(left.at[slot], left_v, local_sem.at[3])
    fetch_right = pltpu.make_async_copy(right.at[slot], right_v, local_sem.at[4])

    barrier = pltpu.get_barrier_semaphore()

    @pl.when(relays)
    def _():
        for dy in FAR_FIRST:
            for dz in FAR_FIRST:
                if dy or dz:
                    peer = {"dp": lax.rem(y + dy, NY) * NXC + xc, "tensor": lax.rem(z + dz, NZ)}
                    pl.semaphore_signal(barrier, inc=1, device_id=peer, device_id_type=MESH)

    @pl.when(handles)
    def _():
        for step in range(1, NXC):
            peer = {"dp": y * NXC + lax.rem(xc + step, NXC)}
            pl.semaphore_signal(barrier, inc=1, device_id=peer, device_id_type=MESH)
        fetch_left.start()
        fetch_right.start()

    row, col = iota((256, 256), 0), iota((256, 256), 1)
    source = (row // 128) * 128 + ((row // 8) % 8) * 16 + (row % 8) * 2 + (row // 64) % 2
    order = one_where(col == source)
    block = iota((NB, NB), 0)
    fetch[0].wait()
    hit = [block == table_v[c : c + 1, :] for c in (0, 1)]
    pick = dot_nt(order, one_where(jnp.concatenate(hit, axis=1))).astype(BF16)
    fetch[1].wait()
    pieces = [dot_nt(pick, grad_v[128 * h : 128 * h + 128, :]).reshape(32, 8, 128) for h in (0, 1)]
    send1[...] = jnp.concatenate(pieces, axis=1).astype(BF16).reshape(PLANES, NY, 16, 128)

    awaited = jnp.where(relays, PLANES * NY - 1 + jnp.where(handles, 7, 8), PLANES * NY)
    pl.semaphore_wait(barrier, awaited)

    def put(source, target, sent_on, lands_on, device):
        pltpu.make_async_remote_copy(
            src_ref=source,
            dst_ref=target,
            send_sem=sent_on,
            recv_sem=lands_on,
            device_id=device,
            device_id_type=MESH,
        ).start()

    def put_unless_here(here, source, target, sent_on, lands_on, device):
        @pl.when(jnp.logical_not(here))
        def _():
            put(source, target, sent_on, lands_on, device)

        @pl.when(here)
        def _():
            pltpu.make_async_copy(source, target, lands_on).start()

    def take(ref, sem):
        pltpu.make_async_copy(ref, ref, sem).wait()

    for dy in FAR_FIRST:
        there = lax.rem(y + dy, NY)
        for plane in (3, 2, 1, 0):
            source, target = send1.at[plane, there], recv1.at[z, y]
            device = {"dp": there * NXC + xc, "tensor": plane}
            if dy:
                put(source, target, send_sem.at[0], piece_sem.at[z], device)
            else:
                put_unless_here(z == plane, source, target, send_sem.at[0], piece_sem.at[z], device)

    fetch[2].wait()
    row, col = iota((256, 256), 0), iota((256, 256), 1)
    order = one_where(col == (row % 2) * 128 + ((row // 2) % 8) * 16 + row // 16)
    live = [hit[c] & (counts_v[0:1, :] > c) for c in (0, 1)]
    place[...] = dot_nt(order, one_where(jnp.concatenate(live, axis=1))).astype(BF16)
    row, col = iota((BLK, BLK), 0), iota((BLK, BLK), 1)
    ungroup[...] = one_where(col == (row % 16) * 32 + (row // 32) * 2 + (row // 16) % 2)

    @pl.when(handles)
    def _():
        rows = one_where(col == (row % 256) * 2 + row // 256)
        p = col % 256
        columns = one_where(row == ((p // 2) % 8) * 64 + (p // 16) * 4 + (p % 2) * 2 + col // 256)
        fetch_left.wait()
        high, low = split(left_v[...])
        left_high[...] = dot(dot(rows, high).astype(BF16), columns).astype(BF16)
        left_low[...] = dot(dot(rows, low).astype(BF16), columns).astype(BF16)
        fetch_right.wait()
        high, low = split(right_v[...])
        right_high[...] = high
        right_low[...] = low

    @pl.when(relays)
    def _():
        row, col = iota((128, 128), 0), iota((128, 128), 1)
        turn = one_where(col == ((row // 2) % 8) * 16 + (row % 2) * 8 + row // 16)
        for t in range(NZ):
            take(recv1.at[t], piece_sem.at[t])
            turned = dot(turn, recv1[t].reshape(128, 128)).astype(BF16)
            send2[t] = turned.reshape(NX, 16, 128)
            for dx in FAR_FIRST:
                there = lax.rem(x + dx, NX)
                source, target = send2.at[t, there], recv2.at[t, xc]
                device = {"dp": y * NXC + there * 2 + lax.rem(z, 2)}
                if dx:
                    put(source, target, send_sem.at[1], panel_sem.at[t], device)
                else:
                    put_unless_here(handles, source, target, send_sem.at[1], panel_sem.at[t], device)

    @pl.when(handles)
    def _():
        def half(u):
            panels = []
            for t in range(4 * u, 4 * u + 4):
                take(recv2.at[t], panel_sem.at[t])
                panels.append(recv2[t].reshape(256, 128))
            even = jnp.concatenate([panel[:, :64] for panel in panels], axis=1)
            odd = jnp.concatenate([panel[:, 64:] for panel in panels], axis=1)
            held = jnp.concatenate([even, odd], axis=0)
            high, low = split(dot(left_high[...], held) + dot(left_low[...], held))
            first, second = right_high[256 * u : 256 * u + 256, :], right_low[256 * u : 256 * u + 256, :]
            wide = held.astype(F32)
            return dot(high, first) + dot(low, first) + dot(high, second), jnp.sum(wide * wide, keepdims=True)

        partial[...], first_sum = half(0)
        rest, second_sum = half(1)
        direction = partial[...] + rest
        entries = BLK * BLK
        grad_mean = (first_sum + second_sum) / entries
        dir_mean = jnp.sum(direction * direction, keepdims=True) / entries
        factor = jnp.sqrt(grad_mean) * lax.rsqrt(dir_mean + EPSILON)
        mine = (iota((1, NB), 1) == dp) & (counts_v[...] > slot)
        alive = jnp.max(jnp.where(mine, 1.0, 0.0), keepdims=True) > 0.0
        update = jnp.where(alive, direction * factor, 0.0).astype(BF16)
        for t in range(0, NZ, 2):
            upper, lower = update[:256, 64 * t : 64 * t + 128], update[256:, 64 * t : 64 * t + 128]
            first = jnp.concatenate([upper[:, :64], lower[:, :64]], axis=1)
            second = jnp.concatenate([upper[:, 64:], lower[:, 64:]], axis=1)
            send3[:, t] = first.reshape(NY, 32, 128)
            send3[:, t + 1] = second.reshape(NY, 32, 128)
            for plane in (t, t + 1):
                for there in EARLY_Y:
                    source, target = send3.at[there, plane], recv3.at[y * 2 + slot]
                    device = {"dp": there * NXC + xc, "tensor": plane}
                    if plane < PLANES:
                        here = (there == y) & (plane == z)
                        put_unless_here(here, source, target, send_sem.at[2], recv_sem.at[0], device)
                    else:
                        put(source, target, send_sem.at[2], recv_sem.at[0], device)

    take(recv3, recv_sem.at[0])
    grouped = dot(ungroup[...], recv3[...].reshape(BLK, 128)).astype(BF16)
    send4[...] = grouped.reshape(NXC, 32, 128)
    for there_x in EARLY_X:
        for there in (there_x * 2 + 1, there_x * 2):
            device = {"dp": y * NXC + there}
            put_unless_here(there == xc, send4.at[there], recv4.at[xc], send_sem.at[3], recv_sem.at[1], device)

    take(recv4, recv_sem.at[1])
    for h in (0, 1):
        returned = recv4[:, 16 * h : 16 * h + 16, :].reshape(256, 128)
        out[128 * h : 128 * h + 128, :] = dot_tn(returned, place[...]).astype(BF16)

    take(send4.at[pl.ds(0, 15)], send_sem.at[3])

    @pl.when(relays)
    def _():
        take(send1.at[pl.ds(0, 3)], send_sem.at[0])
        take(send1.at[3, pl.ds(0, 7)], send_sem.at[0])
        take(send2.at[:, pl.ds(0, 7)], send_sem.at[1])

    @pl.when(jnp.logical_not(relays))
    def _():
        take(send1, send_sem.at[0])

    @pl.when(relays & jnp.logical_not(handles))
    def _():
        take(send2.at[:, 7], send_sem.at[1])

    @pl.when(handles)
    def _():
        take(send3.at[pl.ds(0, 7)], send_sem.at[2])
        take(send3.at[7, pl.ds(0, 7)], send_sem.at[2])


def body(gradient, left_root, right_root, counts, slot_table):
    pieces = jnp.transpose(gradient, (1, 2, 0)).reshape(256, NB)
    vmem = pltpu.VMEM
    message = (32, 128)
    update = pl.pallas_call(
        kernel,
        out_shape=jax.ShapeDtypeStruct((256, NB), BF16),
        in_specs=[pl.BlockSpec(memory_space=pltpu.HBM)] * 5,
        out_specs=pl.BlockSpec(memory_space=pltpu.VMEM),
        scratch_shapes=[
            vmem((256, NB), BF16),
            vmem((BLK, BLK), F32),
            vmem((BLK, BLK), F32),
            vmem((1, NB), jnp.int32),
            vmem((2, NB), jnp.int32),
            vmem((PLANES, NY, 16, 128), BF16),
            vmem((NZ, NY, 16, 128), BF16),
            vmem((NZ, NX, 16, 128), BF16),
            vmem((NZ, NXC, 16, 128), BF16),
            vmem((NY, NZ, *message), BF16),
            vmem((16, *message), BF16),
            vmem((16, *message), BF16),
            vmem((16, *message), BF16),
            vmem((BLK, BLK), BF16),
            vmem((BLK, BLK), BF16),
            vmem((BLK, BLK), BF16),
            vmem((BLK, BLK), BF16),
            vmem((BLK, BLK), BF16),
            vmem((256, NB), BF16),
            vmem((BLK, BLK), F32),
            pltpu.SemaphoreType.DMA((5,)),
            pltpu.SemaphoreType.DMA((4,)),
            pltpu.SemaphoreType.DMA((2,)),
            pltpu.SemaphoreType.DMA((NZ,)),
            pltpu.SemaphoreType.DMA((NZ,)),
        ],
        compiler_params=pltpu.CompilerParams(
            collective_id=0, has_side_effects=True, vmem_limit_bytes=62 * 1024 * 1024
        ),
    )(pieces, left_root, right_root, counts.reshape(1, NB), slot_table.T)
    return jnp.transpose(update.reshape(4, 64, NB), (2, 0, 1))


def solution(mesh):
    return jax.shard_map(
        body,
        mesh=mesh,
        in_specs=(P(None, "dp", "tensor"), P("dp", None, None), P("dp", None, None), P(), P()),
        out_specs=P(None, "dp", "tensor"),
        check_vma=False,
    )
```

```python
import jax
import jax.numpy as jnp
from jax import lax
from jax.experimental import pallas as pl
from jax.experimental.pallas import tpu as pltpu
from jax.sharding import PartitionSpec as P

MESH = pl.DeviceIdType.MESH
EPSILON = 1e-06
BLK = 512
NB = 128
NY, NX, NXC, NZ = 8, 8, 16, 8
F32, BF16 = jnp.float32, jnp.bfloat16
PLANES = 4
FAR_FIRST = (4, 3, 5, 2, 6, 1, 7, 0)
BATCHES = ((0, 4), (4, 2), (6, 2))
EARLY_X = (0, 1, 2, 7, 3, 6, 5, 4)
EARLY_Y = (0, 1, 2, 3, 7, 6, 5, 4)


def iota(shape, dim):
    return lax.broadcasted_iota(jnp.int32, shape, dim)


def one_where(mask):
    return jnp.where(mask, 1.0, 0.0).astype(BF16)


def dot(a, b):
    return jnp.dot(a, b, preferred_element_type=F32)


def dot_nt(a, b):
    return lax.dot_general(a, b, (((1,), (1,)), ((), ())), preferred_element_type=F32)


def dot_tn(a, b):
    return lax.dot_general(a, b, (((0,), (0,)), ((), ())), preferred_element_type=F32)


def split(value):
    high = value.astype(BF16)
    return high, (value - high.astype(F32)).astype(BF16)


def kernel(
    grad, left, right, counts, table, out,
    grad_v, left_v, right_v, counts_v, table_v,
    send1, recv1, send2, recv2, send3, recv3, send4, recv4,
    left_high, left_low, right_high, right_low, ungroup, place, partial,
    local_sem, send_sem, recv_sem, piece_sem, panel_sem,
):
    dp, z = lax.axis_index("dp"), lax.axis_index("tensor")
    y, xc = dp // NXC, lax.rem(dp, NXC)
    x, core = xc // 2, lax.rem(xc, 2)
    slot = lax.rem(z // 2, 2)
    relays = z < PLANES
    handles = relays & (core == lax.rem(z, 2))

    fetch = [
        pltpu.make_async_copy(table, table_v, local_sem.at[0]),
        pltpu.make_async_copy(grad, grad_v, local_sem.at[1]),
        pltpu.make_async_copy(counts, counts_v, local_sem.at[2]),
    ]
    for copy in fetch:
        copy.start()
    fetch_left = pltpu.make_async_copy(left.at[slot], left_v, local_sem.at[3])
    fetch_right = pltpu.make_async_copy(right.at[slot], right_v, local_sem.at[4])

    barrier = pltpu.get_barrier_semaphore()

    @pl.when(relays)
    def _():
        for dy in FAR_FIRST:
            for dz in FAR_FIRST:
                if dy or dz:
                    peer = {"dp": lax.rem(y + dy, NY) * NXC + xc, "tensor": lax.rem(z + dz, NZ)}
                    pl.semaphore_signal(barrier, inc=1, device_id=peer, device_id_type=MESH)

    @pl.when(handles)
    def _():
        for step in range(1, NXC):
            peer = {"dp": y * NXC + lax.rem(xc + step, NXC)}
            pl.semaphore_signal(barrier, inc=1, device_id=peer, device_id_type=MESH)
        fetch_left.start()
        fetch_right.start()

    row, col = iota((256, 256), 0), iota((256, 256), 1)
    source = (row // 128) * 128 + ((row // 8) % 8) * 16 + (row % 8) * 2 + (row // 64) % 2
    order = one_where(col == source)
    block = iota((NB, NB), 0)
    fetch[0].wait()
    hit = [block == table_v[c : c + 1, :] for c in (0, 1)]
    pick = dot_nt(order, one_where(jnp.concatenate(hit, axis=1))).astype(BF16)
    fetch[1].wait()
    pieces = [dot_nt(pick, grad_v[128 * h : 128 * h + 128, :]).reshape(32, 8, 128) for h in (0, 1)]
    send1[...] = jnp.concatenate(pieces, axis=1).astype(BF16).reshape(PLANES, NY, 16, 128)

    def prepare():
        fetch[2].wait()
        row, col = iota((256, 256), 0), iota((256, 256), 1)
        order = one_where(col == (row % 2) * 128 + ((row // 2) % 8) * 16 + row // 16)
        live = [hit[c] & (counts_v[0:1, :] > c) for c in (0, 1)]
        place[...] = dot_nt(order, one_where(jnp.concatenate(live, axis=1))).astype(BF16)
        row, col = iota((BLK, BLK), 0), iota((BLK, BLK), 1)
        ungroup[...] = one_where(col == (row % 16) * 32 + (row // 32) * 2 + (row // 16) % 2)

    pl.when(relays)(prepare)

    @pl.when(handles)
    def _():
        row, col = iota((BLK, BLK), 0), iota((BLK, BLK), 1)
        rows = one_where(col == (row % 256) * 2 + row // 256)
        p = col % 256
        columns = one_where(row == ((p // 2) % 8) * 64 + (p // 16) * 4 + (p % 2) * 2 + col // 256)
        fetch_left.wait()
        high, low = split(left_v[...])
        left_high[...] = dot(dot(rows, high).astype(BF16), columns).astype(BF16)
        left_low[...] = dot(dot(rows, low).astype(BF16), columns).astype(BF16)
        fetch_right.wait()
        high, low = split(right_v[...])
        right_high[...] = high
        right_low[...] = low

    awaited = jnp.where(relays, PLANES * NY - 1 + jnp.where(handles, 7, 8), PLANES * NY)
    pl.semaphore_wait(barrier, awaited)

    def put(source, target, sent_on, lands_on, device):
        pltpu.make_async_remote_copy(
            src_ref=source,
            dst_ref=target,
            send_sem=sent_on,
            recv_sem=lands_on,
            device_id=device,
            device_id_type=MESH,
        ).start()

    def put_unless_here(here, source, target, sent_on, lands_on, device):
        @pl.when(jnp.logical_not(here))
        def _():
            put(source, target, sent_on, lands_on, device)

        @pl.when(here)
        def _():
            pltpu.make_async_copy(source, target, lands_on).start()

    def take(ref, sem):
        pltpu.make_async_copy(ref, ref, sem).wait()

    batch = jnp.where(z < 4, 0, z // 2 - 1)
    for dy in FAR_FIRST:
        there = lax.rem(y + dy, NY)
        for plane in (3, 2, 1, 0):
            source, target = send1.at[plane, there], recv1.at[z, y]
            device = {"dp": there * NXC + xc, "tensor": plane}
            if dy:
                put(source, target, send_sem.at[0], piece_sem.at[batch], device)
            else:
                put_unless_here(z == plane, source, target, send_sem.at[0], piece_sem.at[batch], device)

    pl.when(jnp.logical_not(relays))(prepare)

    @pl.when(relays)
    def _():
        row, col = iota((128, 128), 0), iota((128, 128), 1)
        turn = one_where(col == ((row // 2) % 8) * 16 + (row % 2) * 8 + row // 16)
        for batch, (start, size) in enumerate(BATCHES):
            planes = pl.ds(start, size)
            take(recv1.at[planes], piece_sem.at[batch])
            arrived = [recv1[t].reshape(128, 128) for t in range(start, start + size)]
            turned = dot(turn, jnp.concatenate(arrived, axis=1)).astype(BF16)
            for k in range(size):
                send2[start + k] = turned[:, 128 * k : 128 * k + 128].reshape(NX, 16, 128)
            lands_on = panel_sem.at[start // 4]
            for dx in FAR_FIRST:
                there = lax.rem(x + dx, NX)
                source, target = send2.at[planes, there], recv2.at[planes, xc]
                device = {"dp": y * NXC + there * 2 + lax.rem(z, 2)}
                if dx:
                    put(source, target, send_sem.at[1], lands_on, device)
                else:
                    put_unless_here(handles, source, target, send_sem.at[1], lands_on, device)

    @pl.when(handles)
    def _():
        def half(u):
            take(recv2.at[pl.ds(4 * u, 4)], panel_sem.at[u])
            panels = [recv2[t].reshape(256, 128) for t in range(4 * u, 4 * u + 4)]
            even = jnp.concatenate([panel[:, :64] for panel in panels], axis=1)
            odd = jnp.concatenate([panel[:, 64:] for panel in panels], axis=1)
            held = jnp.concatenate([even, odd], axis=0)
            high, low = split(dot(left_high[...], held) + dot(left_low[...], held))
            first, second = right_high[256 * u : 256 * u + 256, :], right_low[256 * u : 256 * u + 256, :]
            wide = held.astype(F32)
            return dot(high, first) + dot(low, first) + dot(high, second), jnp.sum(wide * wide, keepdims=True)

        partial[...], first_sum = half(0)
        rest, second_sum = half(1)
        direction = partial[...] + rest
        entries = BLK * BLK
        grad_mean = (first_sum + second_sum) / entries
        dir_mean = jnp.sum(direction * direction, keepdims=True) / entries
        factor = jnp.sqrt(grad_mean) * lax.rsqrt(dir_mean + EPSILON)
        mine = (iota((1, NB), 1) == dp) & (counts_v[...] > slot)
        alive = jnp.max(jnp.where(mine, 1.0, 0.0), keepdims=True) > 0.0
        for t in range(0, NZ, 2):
            update = jnp.where(alive, direction[:, 64 * t : 64 * t + 128] * factor, 0.0).astype(BF16)
            upper, lower = update[:256], update[256:]
            first = jnp.concatenate([upper[:, :64], lower[:, :64]], axis=1)
            second = jnp.concatenate([upper[:, 64:], lower[:, 64:]], axis=1)
            send3[:, t] = first.reshape(NY, 32, 128)
            send3[:, t + 1] = second.reshape(NY, 32, 128)
            for plane in (t, t + 1):
                for there in EARLY_Y:
                    source, target = send3.at[there, plane], recv3.at[y * 2 + slot]
                    device = {"dp": there * NXC + xc, "tensor": plane}
                    if plane < PLANES:
                        here = (there == y) & (plane == z)
                        put_unless_here(here, source, target, send_sem.at[2], recv_sem.at[0], device)
                    else:
                        put(source, target, send_sem.at[2], recv_sem.at[0], device)

    take(recv3, recv_sem.at[0])
    grouped = dot(ungroup[...], recv3[...].reshape(BLK, 128)).astype(BF16)
    send4[...] = grouped.reshape(NXC, 32, 128)
    for there_x in EARLY_X:
        for there in (there_x * 2 + 1, there_x * 2):
            device = {"dp": y * NXC + there}
            put_unless_here(there == xc, send4.at[there], recv4.at[xc], send_sem.at[3], recv_sem.at[1], device)

    take(recv4, recv_sem.at[1])
    for h in (0, 1):
        returned = recv4[:, 16 * h : 16 * h + 16, :].reshape(256, 128)
        out[128 * h : 128 * h + 128, :] = dot_tn(returned, place[...]).astype(BF16)

    take(send4.at[pl.ds(0, 15)], send_sem.at[3])

    @pl.when(relays)
    def _():
        take(send1.at[pl.ds(0, 3)], send_sem.at[0])
        take(send1.at[3, pl.ds(0, 7)], send_sem.at[0])
        take(send2.at[:, pl.ds(0, 7)], send_sem.at[1])

    @pl.when(jnp.logical_not(relays))
    def _():
        take(send1, send_sem.at[0])

    @pl.when(relays & jnp.logical_not(handles))
    def _():
        take(send2.at[:, 7], send_sem.at[1])

    @pl.when(handles)
    def _():
        take(send3.at[pl.ds(0, 7)], send_sem.at[2])
        take(send3.at[7, pl.ds(0, 7)], send_sem.at[2])


def body(gradient, left_root, right_root, counts, slot_table):
    pieces = jnp.transpose(gradient, (1, 2, 0)).reshape(256, NB)
    vmem = pltpu.VMEM
    message = (32, 128)
    update = pl.pallas_call(
        kernel,
        out_shape=jax.ShapeDtypeStruct((256, NB), BF16),
        in_specs=[pl.BlockSpec(memory_space=pltpu.HBM)] * 5,
        out_specs=pl.BlockSpec(memory_space=pltpu.VMEM),
        scratch_shapes=[
            vmem((256, NB), BF16),
            vmem((BLK, BLK), F32),
            vmem((BLK, BLK), F32),
            vmem((1, NB), jnp.int32),
            vmem((2, NB), jnp.int32),
            vmem((PLANES, NY, 16, 128), BF16),
            vmem((NZ, NY, 16, 128), BF16),
            vmem((NZ, NX, 16, 128), BF16),
            vmem((NZ, NXC, 16, 128), BF16),
            vmem((NY, NZ, *message), BF16),
            vmem((16, *message), BF16),
            vmem((16, *message), BF16),
            vmem((16, *message), BF16),
            vmem((BLK, BLK), BF16),
            vmem((BLK, BLK), BF16),
            vmem((BLK, BLK), BF16),
            vmem((BLK, BLK), BF16),
            vmem((BLK, BLK), BF16),
            vmem((256, NB), BF16),
            vmem((BLK, BLK), F32),
            pltpu.SemaphoreType.DMA((5,)),
            pltpu.SemaphoreType.DMA((4,)),
            pltpu.SemaphoreType.DMA((2,)),
            pltpu.SemaphoreType.DMA((3,)),
            pltpu.SemaphoreType.DMA((2,)),
        ],
        compiler_params=pltpu.CompilerParams(
            collective_id=0, has_side_effects=True, vmem_limit_bytes=62 * 1024 * 1024
        ),
    )(pieces, left_root, right_root, counts.reshape(1, NB), slot_table.T)
    return jnp.transpose(update.reshape(4, 64, NB), (2, 0, 1))


def solution(mesh):
    return jax.shard_map(
        body,
        mesh=mesh,
        in_specs=(P(None, "dp", "tensor"), P("dp", None, None), P("dp", None, None), P(), P()),
        out_specs=P(None, "dp", "tensor"),
        check_vma=False,
    )
```

```python
import jax
import jax.numpy as jnp
from jax import lax
from jax.experimental import pallas as pl
from jax.experimental.pallas import tpu as pltpu
from jax.sharding import PartitionSpec as P

MESH = pl.DeviceIdType.MESH
EPSILON = 1e-06
BLK = 512
NB = 128
NY, NX, NXC, NZ = 8, 8, 16, 8
F32, BF16 = jnp.float32, jnp.bfloat16
PLANES = 4
FAR_FIRST = (4, 3, 5, 2, 6, 1, 7, 0)
BATCHES = ((0, 4), (4, 2), (6, 2))
EARLY_X = (0, 1, 2, 7, 3, 6, 5, 4)
EARLY_Y = (0, 1, 2, 3, 7, 6, 5, 4)


def iota(shape, dim):
    return lax.broadcasted_iota(jnp.int32, shape, dim)


def one_where(mask):
    return jnp.where(mask, 1.0, 0.0).astype(BF16)


def dot(a, b):
    return jnp.dot(a, b, preferred_element_type=F32)


def dot_nt(a, b):
    return lax.dot_general(a, b, (((1,), (1,)), ((), ())), preferred_element_type=F32)


def dot_tn(a, b):
    return lax.dot_general(a, b, (((0,), (0,)), ((), ())), preferred_element_type=F32)


def split(value):
    high = value.astype(BF16)
    return high, (value - high.astype(F32)).astype(BF16)


def kernel(
    grad, left, right, counts, table, out,
    grad_v, left_v, right_v, counts_v, table_v,
    send1, recv1, send2, recv2, send3, recv3, send4, recv4,
    left_high, left_low, right_high, right_low, ungroup, place, partial,
    local_sem, send_sem, recv_sem, piece_sem, panel_sem,
):
    dp, z = lax.axis_index("dp"), lax.axis_index("tensor")
    y, xc = dp // NXC, lax.rem(dp, NXC)
    x, core = xc // 2, lax.rem(xc, 2)
    slot = lax.rem(z // 2, 2)
    relays = z < PLANES
    handles = relays & (core == lax.rem(z, 2))

    fetch = [
        pltpu.make_async_copy(table, table_v, local_sem.at[0]),
        pltpu.make_async_copy(grad, grad_v, local_sem.at[1]),
        pltpu.make_async_copy(counts, counts_v, local_sem.at[2]),
    ]
    for copy in fetch:
        copy.start()
    fetch_left = pltpu.make_async_copy(left.at[slot], left_v, local_sem.at[3])
    fetch_right = pltpu.make_async_copy(right.at[slot], right_v, local_sem.at[4])

    barrier = pltpu.get_barrier_semaphore()

    @pl.when(relays)
    def _():
        for dy in FAR_FIRST:
            for dz in FAR_FIRST:
                if dy or dz:
                    peer = {"dp": lax.rem(y + dy, NY) * NXC + xc, "tensor": lax.rem(z + dz, NZ)}
                    pl.semaphore_signal(barrier, inc=1, device_id=peer, device_id_type=MESH)

    @pl.when(handles)
    def _():
        for step in range(1, NXC):
            peer = {"dp": y * NXC + lax.rem(xc + step, NXC)}
            pl.semaphore_signal(barrier, inc=1, device_id=peer, device_id_type=MESH)
        fetch_left.start()
        fetch_right.start()

    row, col = iota((256, 256), 0), iota((256, 256), 1)
    source = (row // 128) * 128 + ((row // 8) % 8) * 16 + (row % 8) * 2 + (row // 64) % 2
    order = one_where(col == source)
    block = iota((NB, NB), 0)
    fetch[0].wait()
    hit = [block == table_v[c : c + 1, :] for c in (0, 1)]
    pick = dot_nt(order, one_where(jnp.concatenate(hit, axis=1))).astype(BF16)
    fetch[1].wait()
    pieces = [dot_nt(pick, grad_v[128 * h : 128 * h + 128, :]).reshape(32, 8, 128) for h in (0, 1)]
    send1[...] = jnp.concatenate(pieces, axis=1).astype(BF16).reshape(PLANES, NY, 16, 128)

    def prepare():
        fetch[2].wait()
        row, col = iota((256, 256), 0), iota((256, 256), 1)
        order = one_where(col == (row % 2) * 128 + ((row // 2) % 8) * 16 + row // 16)
        live = [hit[c] & (counts_v[0:1, :] > c) for c in (0, 1)]
        place[...] = dot_nt(order, one_where(jnp.concatenate(live, axis=1))).astype(BF16)
        row, col = iota((BLK, BLK), 0), iota((BLK, BLK), 1)
        ungroup[...] = one_where(col == (row % 16) * 32 + (row // 32) * 2 + (row // 16) % 2)

    pl.when(relays)(prepare)

    @pl.when(handles)
    def _():
        row, col = iota((BLK, BLK), 0), iota((BLK, BLK), 1)
        rows = one_where(col == (row % 256) * 2 + row // 256)
        p = col % 256
        columns = one_where(row == ((p // 2) % 8) * 64 + (p // 16) * 4 + (p % 2) * 2 + col // 256)
        fetch_left.wait()
        high, low = split(left_v[...])
        left_high[...] = dot(dot(rows, high).astype(BF16), columns).astype(BF16)
        left_low[...] = dot(dot(rows, low).astype(BF16), columns).astype(BF16)
        fetch_right.wait()
        high, low = split(right_v[...])
        right_high[...] = high
        right_low[...] = low

    awaited = jnp.where(relays, PLANES * NY - 1 + jnp.where(handles, 7, 8), PLANES * NY)
    pl.semaphore_wait(barrier, awaited)

    def put(source, target, sent_on, lands_on, device):
        pltpu.make_async_remote_copy(
            src_ref=source,
            dst_ref=target,
            send_sem=sent_on,
            recv_sem=lands_on,
            device_id=device,
            device_id_type=MESH,
        ).start()

    def put_unless_here(here, source, target, sent_on, lands_on, device):
        @pl.when(jnp.logical_not(here))
        def _():
            put(source, target, sent_on, lands_on, device)

        @pl.when(here)
        def _():
            pltpu.make_async_copy(source, target, lands_on).start()

    def take(ref, sem):
        pltpu.make_async_copy(ref, ref, sem).wait()

    batch = jnp.where(z < 4, 0, z // 2 - 1)
    for dy in FAR_FIRST:
        there = lax.rem(y + dy, NY)
        for plane in (3, 2, 1, 0):
            source, target = send1.at[plane, there], recv1.at[z, y]
            device = {"dp": there * NXC + xc, "tensor": plane}
            if dy:
                put(source, target, send_sem.at[0], piece_sem.at[batch], device)
            else:
                put_unless_here(z == plane, source, target, send_sem.at[0], piece_sem.at[batch], device)

    pl.when(jnp.logical_not(relays))(prepare)

    @pl.when(relays)
    def _():
        row, col = iota((128, 128), 0), iota((128, 128), 1)
        turn = one_where(col == ((row // 2) % 8) * 16 + (row % 2) * 8 + row // 16)
        for batch, (start, size) in enumerate(BATCHES):
            planes = pl.ds(start, size)
            take(recv1.at[planes], piece_sem.at[batch])
            arrived = [recv1[t].reshape(128, 128) for t in range(start, start + size)]
            turned = dot(turn, jnp.concatenate(arrived, axis=1)).astype(BF16)
            for k in range(size):
                send2[start + k] = turned[:, 128 * k : 128 * k + 128].reshape(NX, 16, 128)
            lands_on = panel_sem.at[start // 4]
            for dx in FAR_FIRST:
                there = lax.rem(x + dx, NX)
                source, target = send2.at[planes, there], recv2.at[planes, xc]
                device = {"dp": y * NXC + there * 2 + lax.rem(z, 2)}
                if dx:
                    put(source, target, send_sem.at[1], lands_on, device)
                else:
                    put_unless_here(handles, source, target, send_sem.at[1], lands_on, device)

    @pl.when(handles)
    def _():
        def half(u):
            take(recv2.at[pl.ds(4 * u, 4)], panel_sem.at[u])
            panels = [recv2[t].reshape(256, 128) for t in range(4 * u, 4 * u + 4)]
            even = jnp.concatenate([panel[:, :64] for panel in panels], axis=1)
            odd = jnp.concatenate([panel[:, 64:] for panel in panels], axis=1)
            held = jnp.concatenate([even, odd], axis=0)
            high, low = split(dot(left_high[...], held) + dot(left_low[...], held))
            first, second = right_high[256 * u : 256 * u + 256, :], right_low[256 * u : 256 * u + 256, :]
            wide = held.astype(F32)
            return dot(high, first) + dot(low, first) + dot(high, second), jnp.sum(wide * wide, keepdims=True)

        partial[...], first_sum = half(0)
        rest, second_sum = half(1)
        direction = partial[...] + rest
        entries = BLK * BLK
        grad_mean = (first_sum + second_sum) / entries
        dir_mean = jnp.sum(direction * direction, keepdims=True) / entries
        factor = jnp.sqrt(grad_mean) * lax.rsqrt(dir_mean + EPSILON)
        mine = (iota((1, NB), 1) == dp) & (counts_v[...] > slot)
        alive = jnp.max(jnp.where(mine, 1.0, 0.0), keepdims=True) > 0.0
        for t in range(0, NZ, 2):
            update = jnp.where(alive, direction[:, 64 * t : 64 * t + 128] * factor, 0.0).astype(BF16)
            upper, lower = update[:256], update[256:]
            first = jnp.concatenate([upper[:, :64], lower[:, :64]], axis=1)
            second = jnp.concatenate([upper[:, 64:], lower[:, 64:]], axis=1)
            send3[:, t] = first.reshape(NY, 32, 128)
            send3[:, t + 1] = second.reshape(NY, 32, 128)
            for plane in (t, t + 1):
                for there in EARLY_Y:
                    source, target = send3.at[there, plane], recv3.at[y * 2 + slot]
                    device = {"dp": there * NXC + xc, "tensor": plane}
                    if plane < PLANES:
                        here = (there == y) & (plane == z)
                        put_unless_here(here, source, target, send_sem.at[2], recv_sem.at[0], device)
                    else:
                        put(source, target, send_sem.at[2], recv_sem.at[0], device)

    take(recv3, recv_sem.at[0])
    grouped = dot(ungroup[...], recv3[...].reshape(BLK, 128)).astype(BF16)
    send4[...] = grouped.reshape(NXC, 32, 128)
    for there_x in EARLY_X:
        for there in (there_x * 2 + 1, there_x * 2):
            device = {"dp": y * NXC + there}
            put_unless_here(there == xc, send4.at[there], recv4.at[xc], send_sem.at[3], recv_sem.at[1], device)

    take(recv4, recv_sem.at[1])
    for h in (0, 1):
        returned = recv4[:, 16 * h : 16 * h + 16, :].reshape(256, 128)
        out[128 * h : 128 * h + 128, :] = dot_tn(returned, place[...]).astype(BF16)

    take(send4.at[pl.ds(0, 15)], send_sem.at[3])

    @pl.when(relays)
    def _():
        take(send1.at[pl.ds(0, 3)], send_sem.at[0])
        take(send1.at[3, pl.ds(0, 7)], send_sem.at[0])
        take(send2.at[:, pl.ds(0, 7)], send_sem.at[1])

    @pl.when(jnp.logical_not(relays))
    def _():
        take(send1, send_sem.at[0])

    @pl.when(relays & jnp.logical_not(handles))
    def _():
        take(send2.at[:, 7], send_sem.at[1])

    @pl.when(handles)
    def _():
        take(send3.at[pl.ds(0, 7)], send_sem.at[2])
        take(send3.at[7, pl.ds(0, 7)], send_sem.at[2])


def body(gradient, left_root, right_root, counts, slot_table):
    pieces = jnp.transpose(gradient, (1, 2, 0)).reshape(256, NB)
    operands = (pieces, left_root, right_root, counts.reshape(1, NB), slot_table.T)
    operands = [pltpu.with_memory_space_constraint(operand, pltpu.HBM) for operand in operands]
    vmem = pltpu.VMEM
    message = (32, 128)
    update = pl.pallas_call(
        kernel,
        out_shape=jax.ShapeDtypeStruct((256, NB), BF16),
        in_specs=[pl.BlockSpec(memory_space=pltpu.HBM)] * 5,
        out_specs=pl.BlockSpec(memory_space=pltpu.VMEM),
        scratch_shapes=[
            vmem((256, NB), BF16),
            vmem((BLK, BLK), F32),
            vmem((BLK, BLK), F32),
            vmem((1, NB), jnp.int32),
            vmem((2, NB), jnp.int32),
            vmem((PLANES, NY, 16, 128), BF16),
            vmem((NZ, NY, 16, 128), BF16),
            vmem((NZ, NX, 16, 128), BF16),
            vmem((NZ, NXC, 16, 128), BF16),
            vmem((NY, NZ, *message), BF16),
            vmem((16, *message), BF16),
            vmem((16, *message), BF16),
            vmem((16, *message), BF16),
            vmem((BLK, BLK), BF16),
            vmem((BLK, BLK), BF16),
            vmem((BLK, BLK), BF16),
            vmem((BLK, BLK), BF16),
            vmem((BLK, BLK), BF16),
            vmem((256, NB), BF16),
            vmem((BLK, BLK), F32),
            pltpu.SemaphoreType.DMA((5,)),
            pltpu.SemaphoreType.DMA((4,)),
            pltpu.SemaphoreType.DMA((2,)),
            pltpu.SemaphoreType.DMA((3,)),
            pltpu.SemaphoreType.DMA((2,)),
        ],
        compiler_params=pltpu.CompilerParams(
            collective_id=0, has_side_effects=True, vmem_limit_bytes=40 * 1024 * 1024
        ),
    )(*operands)
    return jnp.transpose(update.reshape(4, 64, NB), (2, 0, 1))


def solution(mesh):
    return jax.shard_map(
        body,
        mesh=mesh,
        in_specs=(P(None, "dp", "tensor"), P("dp", None, None), P("dp", None, None), P(), P()),
        out_specs=P(None, "dp", "tensor"),
        check_vma=False,
    )
```

```python
import jax
import jax.numpy as jnp
from jax import lax
from jax.experimental import pallas as pl
from jax.experimental.pallas import tpu as pltpu
from jax.sharding import PartitionSpec as P

MESH = pl.DeviceIdType.MESH
EPSILON = 1e-06
BLK = 512
NB = 128
NY, NX, NXC, NZ = 8, 8, 16, 8
F32, BF16 = jnp.float32, jnp.bfloat16
PLANES = 4
FAR_FIRST = (4, 3, 5, 2, 6, 1, 7, 0)
BATCHES = ((0, 4), (4, 2), (6, 2))
EARLY_X = (0, 1, 2, 7, 3, 6, 5, 4)
EARLY_Y = (0, 1, 2, 3, 7, 6, 5, 4)


def iota(shape, dim):
    return lax.broadcasted_iota(jnp.int32, shape, dim)


def one_where(mask):
    return jnp.where(mask, 1.0, 0.0).astype(BF16)


def reorder(n, place_of):
    return one_where(iota((n, n), 0) == place_of(iota((1, n), 1)))


def dot(a, b):
    return jnp.dot(a, b, preferred_element_type=F32)


def dot_nt(a, b):
    return lax.dot_general(a, b, (((1,), (1,)), ((), ())), preferred_element_type=F32)


def dot_tn(a, b):
    return lax.dot_general(a, b, (((0,), (0,)), ((), ())), preferred_element_type=F32)


def split(value):
    high = value.astype(BF16)
    return high, (value - high.astype(F32)).astype(BF16)


def kernel(
    grad, left, right, counts, table, out,
    grad_v, left_v, right_v, counts_v, table_v,
    send1, recv1, send2, recv2, send3, recv3, send4, recv4,
    left_high, left_low, right_high, right_low, ungroup, place, partial,
    local_sem, send_sem, recv_sem, piece_sem, panel_sem,
):
    dp, z = lax.axis_index("dp"), lax.axis_index("tensor")
    y, xc = dp // NXC, lax.rem(dp, NXC)
    x, core = xc // 2, lax.rem(xc, 2)
    slot = lax.rem(z // 2, 2)
    relays = z < PLANES
    handles = relays & (core == lax.rem(z, 2))

    fetch = [
        pltpu.make_async_copy(table, table_v, local_sem.at[0]),
        pltpu.make_async_copy(grad, grad_v, local_sem.at[1]),
        pltpu.make_async_copy(counts, counts_v, local_sem.at[2]),
    ]
    for copy in fetch:
        copy.start()
    fetch_left = pltpu.make_async_copy(left.at[slot], left_v, local_sem.at[3])
    fetch_right = pltpu.make_async_copy(right.at[slot], right_v, local_sem.at[4])

    barrier = pltpu.get_barrier_semaphore()

    @pl.when(relays)
    def _():
        for dy in FAR_FIRST:
            for dz in FAR_FIRST:
                if dy or dz:
                    peer = {"dp": lax.rem(y + dy, NY) * NXC + xc, "tensor": lax.rem(z + dz, NZ)}
                    pl.semaphore_signal(barrier, inc=1, device_id=peer, device_id_type=MESH)

    @pl.when(handles)
    def _():
        for step in range(1, NXC):
            peer = {"dp": y * NXC + lax.rem(xc + step, NXC)}
            pl.semaphore_signal(barrier, inc=1, device_id=peer, device_id_type=MESH)
        fetch_left.start()
        fetch_right.start()

    order = reorder(256, lambda k: (k & 128) + ((k & 1) << 6) + (((k >> 4) & 7) << 3) + ((k >> 1) & 7))
    block = iota((NB, NB), 0)
    fetch[0].wait()
    hit = [block == table_v[c : c + 1, :] for c in (0, 1)]
    pick = dot_nt(order, one_where(jnp.concatenate(hit, axis=1))).astype(BF16)
    fetch[1].wait()
    pieces = [dot_nt(pick, grad_v[128 * h : 128 * h + 128, :]).reshape(32, 8, 128) for h in (0, 1)]
    send1[...] = jnp.concatenate(pieces, axis=1).astype(BF16).reshape(PLANES, NY, 16, 128)

    def prepare():
        fetch[2].wait()
        by_owner = reorder(256, lambda k: ((k & 15) << 4) + (((k >> 4) & 7) << 1) + (k >> 7))
        live = [hit[c] & (counts_v[0:1, :] > c) for c in (0, 1)]
        place[...] = dot_nt(by_owner, one_where(jnp.concatenate(live, axis=1))).astype(BF16)
        ungroup[...] = reorder(BLK, lambda k: (((k >> 1) & 15) << 5) + ((k & 1) << 4) + (k >> 5))

    pl.when(relays)(prepare)

    @pl.when(handles)
    def _():
        rows = reorder(BLK, lambda k: ((k & 1) << 8) + (k >> 1))
        columns = reorder(BLK, lambda k: (((k >> 1) & 7) << 6) + (((k >> 4) & 15) << 2) + ((k & 1) << 1) + (k >> 8))
        fetch_left.wait()
        high, low = split(left_v[...])
        left_high[...] = dot(dot(rows, high).astype(BF16), columns).astype(BF16)
        left_low[...] = dot(dot(rows, low).astype(BF16), columns).astype(BF16)
        fetch_right.wait()
        high, low = split(right_v[...])
        right_high[...] = high
        right_low[...] = low

    awaited = jnp.where(relays, PLANES * NY - 1 + jnp.where(handles, 7, 8), PLANES * NY)
    pl.semaphore_wait(barrier, awaited)

    def put(source, target, sent_on, lands_on, device):
        pltpu.make_async_remote_copy(
            src_ref=source,
            dst_ref=target,
            send_sem=sent_on,
            recv_sem=lands_on,
            device_id=device,
            device_id_type=MESH,
        ).start()

    def put_unless_here(here, *args):
        @pl.when(jnp.logical_not(here))
        def _():
            put(*args)

    def put_here(source, target, lands_on):
        pltpu.make_async_copy(source, target, lands_on).start()

    def take(ref, sem):
        pltpu.make_async_copy(ref, ref, sem).wait()

    batch = jnp.where(z < 4, 0, z // 2 - 1)
    for dy in FAR_FIRST:
        there = lax.rem(y + dy, NY)
        for plane in (3, 2, 1, 0):
            source, target = send1.at[plane, there], recv1.at[z, y]
            device = {"dp": there * NXC + xc, "tensor": plane}
            if dy:
                put(source, target, send_sem.at[0], piece_sem.at[batch], device)
            else:
                put_unless_here(z == plane, source, target, send_sem.at[0], piece_sem.at[batch], device)

    pl.when(jnp.logical_not(relays))(prepare)

    @pl.when(relays)
    def _():
        put_here(send1.at[lax.rem(z, PLANES), y], recv1.at[z, y], piece_sem.at[0])
        turn = reorder(128, lambda k: ((k & 7) << 4) + ((k >> 4) << 1) + ((k >> 3) & 1))
        for batch, (start, size) in enumerate(BATCHES):
            planes = pl.ds(start, size)
            take(recv1.at[planes], piece_sem.at[batch])
            arrived = [recv1[t].reshape(128, 128) for t in range(start, start + size)]
            turned = dot(turn, jnp.concatenate(arrived, axis=1)).astype(BF16)
            for k in range(size):
                send2[start + k] = turned[:, 128 * k : 128 * k + 128].reshape(NX, 16, 128)
            lands_on = panel_sem.at[start // 4]
            for dx in FAR_FIRST:
                there = lax.rem(x + dx, NX)
                source, target = send2.at[planes, there], recv2.at[planes, xc]
                device = {"dp": y * NXC + there * 2 + lax.rem(z, 2)}
                if dx:
                    put(source, target, send_sem.at[1], lands_on, device)
                else:
                    put_unless_here(handles, source, target, send_sem.at[1], lands_on, device)

                    @pl.when(handles)
                    def _(source=source, target=target, lands_on=lands_on):
                        put_here(source, target, lands_on)

    @pl.when(handles)
    def _():
        def half(u):
            take(recv2.at[pl.ds(4 * u, 4)], panel_sem.at[u])
            panels = [recv2[t].reshape(256, 128) for t in range(4 * u, 4 * u + 4)]
            even = jnp.concatenate([panel[:, :64] for panel in panels], axis=1)
            odd = jnp.concatenate([panel[:, 64:] for panel in panels], axis=1)
            held = jnp.concatenate([even, odd], axis=0)
            high, low = split(dot(left_high[...], held) + dot(left_low[...], held))
            first, second = right_high[256 * u : 256 * u + 256, :], right_low[256 * u : 256 * u + 256, :]
            wide = held.astype(F32)
            return dot(high, first) + dot(low, first) + dot(high, second), jnp.sum(wide * wide, keepdims=True)

        partial[...], first_sum = half(0)
        rest, second_sum = half(1)
        direction = partial[...] + rest
        entries = BLK * BLK
        grad_mean = (first_sum + second_sum) / entries
        dir_mean = jnp.sum(direction * direction, keepdims=True) / entries
        factor = jnp.sqrt(grad_mean) * lax.rsqrt(dir_mean + EPSILON)
        mine = (iota((1, NB), 1) == dp) & (counts_v[...] > slot)
        alive = jnp.max(jnp.where(mine, 1.0, 0.0), keepdims=True) > 0.0
        for t in range(0, NZ, 2):
            update = jnp.where(alive, direction[:, 64 * t : 64 * t + 128] * factor, 0.0).astype(BF16)
            upper, lower = update[:256], update[256:]
            first = jnp.concatenate([upper[:, :64], lower[:, :64]], axis=1)
            second = jnp.concatenate([upper[:, 64:], lower[:, 64:]], axis=1)
            send3[:, t] = first.reshape(NY, 32, 128)
            send3[:, t + 1] = second.reshape(NY, 32, 128)
            for plane in (t, t + 1):
                for there in EARLY_Y:
                    source, target = send3.at[there, plane], recv3.at[y * 2 + slot]
                    device = {"dp": there * NXC + xc, "tensor": plane}
                    if plane < PLANES:
                        here = (there == y) & (plane == z)
                        put_unless_here(here, source, target, send_sem.at[2], recv_sem.at[0], device)
                    else:
                        put(source, target, send_sem.at[2], recv_sem.at[0], device)
            if t < PLANES:

                @pl.when(slot == t // 2)
                def _():
                    put_here(send3.at[y, lax.rem(z, PLANES)], recv3.at[y * 2 + slot], recv_sem.at[0])

    take(recv3, recv_sem.at[0])
    grouped = dot(ungroup[...], recv3[...].reshape(BLK, 128)).astype(BF16)
    send4[...] = grouped.reshape(NXC, 32, 128)
    for there_x in EARLY_X:
        for there in (there_x * 2 + 1, there_x * 2):
            device = {"dp": y * NXC + there}
            put_unless_here(there == xc, send4.at[there], recv4.at[xc], send_sem.at[3], recv_sem.at[1], device)
    put_here(send4.at[xc], recv4.at[xc], recv_sem.at[1])

    take(recv4, recv_sem.at[1])
    for h in (0, 1):
        returned = recv4[:, 16 * h : 16 * h + 16, :].reshape(256, 128)
        out[128 * h : 128 * h + 128, :] = dot_tn(returned, place[...]).astype(BF16)

    take(send4.at[pl.ds(0, 15)], send_sem.at[3])

    @pl.when(relays)
    def _():
        take(send1.at[pl.ds(0, 3)], send_sem.at[0])
        take(send1.at[3, pl.ds(0, 7)], send_sem.at[0])
        take(send2.at[:, pl.ds(0, 7)], send_sem.at[1])

    @pl.when(jnp.logical_not(relays))
    def _():
        take(send1, send_sem.at[0])

    @pl.when(relays & jnp.logical_not(handles))
    def _():
        take(send2.at[:, 7], send_sem.at[1])

    @pl.when(handles)
    def _():
        take(send3.at[pl.ds(0, 7)], send_sem.at[2])
        take(send3.at[7, pl.ds(0, 7)], send_sem.at[2])


def body(gradient, left_root, right_root, counts, slot_table):
    pieces = jnp.transpose(gradient, (1, 2, 0)).reshape(256, NB)
    operands = (pieces, left_root, right_root, counts.reshape(1, NB), slot_table.T)
    operands = [pltpu.with_memory_space_constraint(operand, pltpu.HBM) for operand in operands]
    vmem = pltpu.VMEM
    message = (32, 128)
    update = pl.pallas_call(
        kernel,
        out_shape=jax.ShapeDtypeStruct((256, NB), BF16),
        in_specs=[pl.BlockSpec(memory_space=pltpu.HBM)] * 5,
        out_specs=pl.BlockSpec(memory_space=pltpu.VMEM),
        scratch_shapes=[
            vmem((256, NB), BF16),
            vmem((BLK, BLK), F32),
            vmem((BLK, BLK), F32),
            vmem((1, NB), jnp.int32),
            vmem((2, NB), jnp.int32),
            vmem((PLANES, NY, 16, 128), BF16),
            vmem((NZ, NY, 16, 128), BF16),
            vmem((NZ, NX, 16, 128), BF16),
            vmem((NZ, NXC, 16, 128), BF16),
            vmem((NY, NZ, *message), BF16),
            vmem((16, *message), BF16),
            vmem((16, *message), BF16),
            vmem((16, *message), BF16),
            vmem((BLK, BLK), BF16),
            vmem((BLK, BLK), BF16),
            vmem((BLK, BLK), BF16),
            vmem((BLK, BLK), BF16),
            vmem((BLK, BLK), BF16),
            vmem((256, NB), BF16),
            vmem((BLK, BLK), F32),
            pltpu.SemaphoreType.DMA((5,)),
            pltpu.SemaphoreType.DMA((4,)),
            pltpu.SemaphoreType.DMA((2,)),
            pltpu.SemaphoreType.DMA((3,)),
            pltpu.SemaphoreType.DMA((2,)),
        ],
        compiler_params=pltpu.CompilerParams(
            collective_id=0, has_side_effects=True, vmem_limit_bytes=40 * 1024 * 1024
        ),
    )(*operands)
    return jnp.transpose(update.reshape(4, 64, NB), (2, 0, 1))


def solution(mesh):
    return jax.shard_map(
        body,
        mesh=mesh,
        in_specs=(P(None, "dp", "tensor"), P("dp", None, None), P("dp", None, None), P(), P()),
        out_specs=P(None, "dp", "tensor"),
        check_vma=False,
    )
```

```python
import jax
import jax.numpy as jnp
from jax import lax
from jax.experimental import pallas as pl
from jax.experimental.pallas import tpu as pltpu
from jax.sharding import PartitionSpec as P

MESH = pl.DeviceIdType.MESH
EPSILON = 1e-06
BLK = 512
NB = 128
NY, NX, NXC, NZ = 8, 8, 16, 8
F32, BF16 = jnp.float32, jnp.bfloat16
PLANES = 4
FAR_FIRST = (4, 3, 5, 2, 6, 1, 7, 0)
BATCHES = ((0, 4), (4, 2), (6, 2))
EARLY_X = (0, 1, 2, 7, 3, 6, 5, 4)
EARLY_Y = (0, 1, 2, 3, 7, 6, 5, 4)


def iota(shape, dim):
    return lax.broadcasted_iota(jnp.int32, shape, dim)


def one_where(mask):
    return jnp.where(mask, 1.0, 0.0).astype(BF16)


def reorder(n, place_of, rows=None):
    return one_where(iota((rows or n, n), 0) == place_of(iota((1, n), 1)))


def dot(a, b):
    return jnp.dot(a, b, preferred_element_type=F32)


def dot_nt(a, b):
    return lax.dot_general(a, b, (((1,), (1,)), ((), ())), preferred_element_type=F32)


def dot_tn(a, b):
    return lax.dot_general(a, b, (((0,), (0,)), ((), ())), preferred_element_type=F32)


def split(value):
    high = value.astype(BF16)
    return high, (value - high.astype(F32)).astype(BF16)


def kernel(
    grad, left, right, counts, table, out,
    grad_v, left_v, right_v, counts_v, table_v,
    send1, recv1, send2, recv2, send3, recv3, send4, recv4,
    left_high, left_low, right_high, right_low, ungroup, place, partial,
    local_sem, send_sem, recv_sem, piece_sem, panel_sem,
):
    dp, z = lax.axis_index("dp"), lax.axis_index("tensor")
    y, xc = dp // NXC, lax.rem(dp, NXC)
    x, core = xc // 2, lax.rem(xc, 2)
    slot = lax.rem(z // 2, 2)
    relays = z < PLANES
    handles = relays & (core == lax.rem(z, 2))

    fetch = [
        pltpu.make_async_copy(table, table_v, local_sem.at[0]),
        pltpu.make_async_copy(grad, grad_v, local_sem.at[1]),
        pltpu.make_async_copy(counts, counts_v, local_sem.at[2]),
    ]
    for copy in fetch:
        copy.start()
    fetch_left = pltpu.make_async_copy(left.at[slot], left_v, local_sem.at[3])
    fetch_right = pltpu.make_async_copy(right.at[slot], right_v, local_sem.at[4])

    barrier = pltpu.get_barrier_semaphore()

    @pl.when(relays)
    def _():
        for dy in FAR_FIRST:
            for dz in FAR_FIRST:
                if dy or dz:
                    peer = {"dp": lax.rem(y + dy, NY) * NXC + xc, "tensor": lax.rem(z + dz, NZ)}
                    pl.semaphore_signal(barrier, inc=1, device_id=peer, device_id_type=MESH)

    @pl.when(handles)
    def _():
        for step in range(1, NXC):
            peer = {"dp": y * NXC + lax.rem(xc + step, NXC)}
            pl.semaphore_signal(barrier, inc=1, device_id=peer, device_id_type=MESH)
        fetch_left.start()
        fetch_right.start()

    order = reorder(256, lambda k: (k & 128) + ((k & 1) << 6) + (((k >> 4) & 7) << 3) + ((k >> 1) & 7))
    block = iota((NB, NB), 0)
    fetch[0].wait()
    hit = [block == table_v[c : c + 1, :] for c in (0, 1)]
    pick = dot_nt(order, one_where(jnp.concatenate(hit, axis=1))).astype(BF16)
    fetch[1].wait()
    pieces = [dot_nt(pick, grad_v[128 * h : 128 * h + 128, :]).reshape(32, 8, 128) for h in (0, 1)]
    send1[...] = jnp.concatenate(pieces, axis=1).astype(BF16).reshape(PLANES, NY, 16, 128)

    def prepare():
        fetch[2].wait()
        for c in (0, 1):
            live = one_where(hit[c] & (counts_v[0:1, :] > c))
            for h in (0, 1):
                by_owner = reorder(NB, lambda k: ((k & 15) << 4) + (h << 3) + (k >> 4), 256)
                place[c, h] = dot_nt(by_owner, live).astype(BF16)
        ungroup[...] = reorder(256, lambda k: (((k >> 1) & 15) << 4) + ((k & 1) << 3) + (k >> 5))

    pl.when(relays)(prepare)

    @pl.when(handles)
    def _():
        rows = reorder(BLK, lambda k: ((k & 1) << 8) + (k >> 1))
        columns = reorder(BLK, lambda k: (((k >> 1) & 7) << 6) + (((k >> 4) & 15) << 2) + ((k & 1) << 1) + (k >> 8))
        fetch_left.wait()
        high, low = split(left_v[...])
        left_high[...] = dot(dot(rows, high).astype(BF16), columns).astype(BF16)
        left_low[...] = dot(dot(rows, low).astype(BF16), columns).astype(BF16)
        fetch_right.wait()
        high, low = split(right_v[...])
        right_high[...] = high
        right_low[...] = low

    awaited = jnp.where(relays, PLANES * NY - 1 + jnp.where(handles, 7, 8), PLANES * NY)
    pl.semaphore_wait(barrier, awaited)

    def put(source, target, sent_on, lands_on, device):
        pltpu.make_async_remote_copy(
            src_ref=source,
            dst_ref=target,
            send_sem=sent_on,
            recv_sem=lands_on,
            device_id=device,
            device_id_type=MESH,
        ).start()

    def put_unless_here(here, source, target, sent_on, lands_on, device):
        @pl.when(jnp.logical_not(here))
        def _():
            put(source, target, sent_on, lands_on, device)

        @pl.when(here)
        def _():
            pltpu.make_async_copy(source, target, lands_on).start()

    def take(ref, sem):
        pltpu.make_async_copy(ref, ref, sem).wait()

    batch = jnp.where(z < 4, 0, z // 2 - 1)
    for dy in FAR_FIRST:
        there = lax.rem(y + dy, NY)
        for plane in (3, 2, 1, 0):
            source, target = send1.at[plane, there], recv1.at[z, y]
            device = {"dp": there * NXC + xc, "tensor": plane}
            if dy:
                put(source, target, send_sem.at[0], piece_sem.at[batch], device)
            else:
                put_unless_here(z == plane, source, target, send_sem.at[0], piece_sem.at[batch], device)

    pl.when(jnp.logical_not(relays))(prepare)

    @pl.when(relays)
    def _():
        turn = reorder(128, lambda k: ((k & 7) << 4) + ((k >> 4) << 1) + ((k >> 3) & 1))
        for batch, (start, size) in enumerate(BATCHES):
            planes = pl.ds(start, size)
            take(recv1.at[planes], piece_sem.at[batch])
            arrived = [recv1[t].reshape(128, 128) for t in range(start, start + size)]
            turned = dot(turn, jnp.concatenate(arrived, axis=1)).astype(BF16)
            for k in range(size):
                send2[start + k] = turned[:, 128 * k : 128 * k + 128].reshape(NX, 16, 128)
            lands_on = panel_sem.at[start // 4]
            for dx in FAR_FIRST:
                there = lax.rem(x + dx, NX)
                source, target = send2.at[planes, there], recv2.at[planes, xc]
                device = {"dp": y * NXC + there * 2 + lax.rem(z, 2)}
                if dx:
                    put(source, target, send_sem.at[1], lands_on, device)
                else:
                    put_unless_here(handles, source, target, send_sem.at[1], lands_on, device)

    @pl.when(handles)
    def _():
        def half(u):
            take(recv2.at[pl.ds(4 * u, 4)], panel_sem.at[u])
            panels = [recv2[t].reshape(256, 128) for t in range(4 * u, 4 * u + 4)]
            even = jnp.concatenate([panel[:, :64] for panel in panels], axis=1)
            odd = jnp.concatenate([panel[:, 64:] for panel in panels], axis=1)
            held = jnp.concatenate([even, odd], axis=0)
            high, low = split(dot(left_high[...], held) + dot(left_low[...], held))
            first, second = right_high[256 * u : 256 * u + 256, :], right_low[256 * u : 256 * u + 256, :]
            wide = held.astype(F32)
            return dot(high, first) + dot(low, first) + dot(high, second), jnp.sum(wide * wide, keepdims=True)

        partial[...], first_sum = half(0)
        rest, second_sum = half(1)
        direction = partial[...] + rest
        entries = BLK * BLK
        grad_mean = (first_sum + second_sum) / entries
        dir_mean = jnp.sum(direction * direction, keepdims=True) / entries
        factor = jnp.sqrt(grad_mean) * lax.rsqrt(dir_mean + EPSILON)
        mine = (iota((1, NB), 1) == dp) & (counts_v[...] > slot)
        alive = jnp.max(jnp.where(mine, 1.0, 0.0), keepdims=True) > 0.0
        for t in range(0, NZ, 2):
            update = jnp.where(alive, direction[:, 64 * t : 64 * t + 128] * factor, 0.0).astype(BF16)
            upper, lower = update[:256], update[256:]
            first = jnp.concatenate([upper[:, :64], lower[:, :64]], axis=1)
            second = jnp.concatenate([upper[:, 64:], lower[:, 64:]], axis=1)
            send3[:, t] = first.reshape(NY, 32, 128)
            send3[:, t + 1] = second.reshape(NY, 32, 128)
            for plane in (t, t + 1):
                for there in EARLY_Y:
                    source, target = send3.at[there, plane], recv3.at[slot, y]
                    device = {"dp": there * NXC + xc, "tensor": plane}
                    if plane < PLANES:
                        here = (there == y) & (plane == z)
                        put_unless_here(here, source, target, send_sem.at[2], recv_sem.at[slot], device)
                    else:
                        put(source, target, send_sem.at[2], recv_sem.at[slot], device)

    for c in (0, 1):
        take(recv3.at[c], recv_sem.at[c])
        grouped = dot(ungroup[...], recv3[c].reshape(256, 128)).astype(BF16)
        send4[c] = grouped.reshape(NXC, 16, 128)
        for there_x in EARLY_X:
            for there in (there_x * 2 + 1, there_x * 2):
                source, target, lands_on = send4.at[c, there], recv4.at[c, xc], recv_sem.at[2 + c]
                device = {"dp": y * NXC + there}
                put_unless_here(there == xc, source, target, send_sem.at[3], lands_on, device)

    halves = [jnp.zeros((128, NB), F32)] * 2
    for c in (0, 1):
        take(recv4.at[c], recv_sem.at[2 + c])
        returned = recv4[c].reshape(256, 128)
        halves = [halves[h] + dot_tn(returned, place[c, h]) for h in (0, 1)]
    out[...] = jnp.concatenate(halves, axis=0).astype(BF16)

    take(send4.at[:, pl.ds(0, 15)], send_sem.at[3])

    @pl.when(relays)
    def _():
        take(send1.at[pl.ds(0, 3)], send_sem.at[0])
        take(send1.at[3, pl.ds(0, 7)], send_sem.at[0])
        take(send2.at[:, pl.ds(0, 7)], send_sem.at[1])

    @pl.when(jnp.logical_not(relays))
    def _():
        take(send1, send_sem.at[0])

    @pl.when(relays & jnp.logical_not(handles))
    def _():
        take(send2.at[:, 7], send_sem.at[1])

    @pl.when(handles)
    def _():
        take(send3.at[pl.ds(0, 7)], send_sem.at[2])
        take(send3.at[7, pl.ds(0, 7)], send_sem.at[2])


def body(gradient, left_root, right_root, counts, slot_table):
    pieces = jnp.transpose(gradient, (1, 2, 0)).reshape(256, NB)
    operands = (pieces, left_root, right_root, counts.reshape(1, NB), slot_table.T)
    operands = [pltpu.with_memory_space_constraint(operand, pltpu.HBM) for operand in operands]
    vmem = pltpu.VMEM
    message = (32, 128)
    update = pl.pallas_call(
        kernel,
        out_shape=jax.ShapeDtypeStruct((256, NB), BF16),
        in_specs=[pl.BlockSpec(memory_space=pltpu.HBM)] * 5,
        out_specs=pl.BlockSpec(memory_space=pltpu.VMEM),
        scratch_shapes=[
            vmem((256, NB), BF16),
            vmem((BLK, BLK), F32),
            vmem((BLK, BLK), F32),
            vmem((1, NB), jnp.int32),
            vmem((2, NB), jnp.int32),
            vmem((PLANES, NY, 16, 128), BF16),
            vmem((NZ, NY, 16, 128), BF16),
            vmem((NZ, NX, 16, 128), BF16),
            vmem((NZ, NXC, 16, 128), BF16),
            vmem((NY, NZ, *message), BF16),
            vmem((2, NY, *message), BF16),
            vmem((2, NXC, 16, 128), BF16),
            vmem((2, NXC, 16, 128), BF16),
            vmem((BLK, BLK), BF16),
            vmem((BLK, BLK), BF16),
            vmem((BLK, BLK), BF16),
            vmem((BLK, BLK), BF16),
            vmem((256, 256), BF16),
            vmem((2, 2, 256, NB), BF16),
            vmem((BLK, BLK), F32),
            pltpu.SemaphoreType.DMA((5,)),
            pltpu.SemaphoreType.DMA((4,)),
            pltpu.SemaphoreType.DMA((4,)),
            pltpu.SemaphoreType.DMA((3,)),
            pltpu.SemaphoreType.DMA((2,)),
        ],
        compiler_params=pltpu.CompilerParams(
            collective_id=0, has_side_effects=True, vmem_limit_bytes=40 * 1024 * 1024
        ),
    )(*operands)
    return jnp.transpose(update.reshape(4, 64, NB), (2, 0, 1))


def solution(mesh):
    return jax.shard_map(
        body,
        mesh=mesh,
        in_specs=(P(None, "dp", "tensor"), P("dp", None, None), P("dp", None, None), P(), P()),
        out_specs=P(None, "dp", "tensor"),
        check_vma=False,
    )
```

```python
import jax
import jax.numpy as jnp
from jax import lax
from jax.experimental import pallas as pl
from jax.experimental.pallas import tpu as pltpu
from jax.sharding import PartitionSpec as P

MESH = pl.DeviceIdType.MESH
EPSILON = 1e-06
BLK = 512
NB = 128
NY, NX, NXC, NZ = 8, 8, 16, 8
F32, BF16 = jnp.float32, jnp.bfloat16
PLANES = 4
FAR_FIRST = (4, 3, 5, 2, 6, 1, 7, 0)
YZ_STEPS = sorted(((dy, dz) for dy in range(8) for dz in range(8)), key=lambda s: -min(s[0], 8 - s[0]) - min(s[1], 8 - s[1]))
BATCHES = ((0, 4), (4, 2), (6, 2))
EARLY_X = (0, 1, 2, 7, 3, 6, 5, 4)
EARLY_Y = (0, 1, 2, 3, 7, 6, 5, 4)


def iota(shape, dim):
    return lax.broadcasted_iota(jnp.int32, shape, dim)


def one_where(mask):
    return jnp.where(mask, 1.0, 0.0).astype(BF16)


def reorder(n, place_of, rows=None):
    return one_where(iota((rows or n, n), 0) == place_of(iota((1, n), 1)))


def dot(a, b):
    return jnp.dot(a, b, preferred_element_type=F32)


def dot_nt(a, b):
    return lax.dot_general(a, b, (((1,), (1,)), ((), ())), preferred_element_type=F32)


def dot_tn(a, b):
    return lax.dot_general(a, b, (((0,), (0,)), ((), ())), preferred_element_type=F32)


def split(value):
    high = value.astype(BF16)
    return high, (value - high.astype(F32)).astype(BF16)


def kernel(
    grad, left, right, counts, table, out,
    grad_v, left_v, right_v, counts_v, table_v,
    send1, recv1, send2, recv2, send3, recv3, send4, recv4,
    left_high, left_low, right_high, right_low, ungroup, place, partial,
    local_sem, send_sem, recv_sem, piece_sem, panel_sem,
):
    dp, z = lax.axis_index("dp"), lax.axis_index("tensor")
    y, xc = dp // NXC, lax.rem(dp, NXC)
    x, core = xc // 2, lax.rem(xc, 2)
    slot = lax.rem(z // 2, 2)
    relays = z < PLANES
    handles = relays & (core == lax.rem(z, 2))

    fetch = [
        pltpu.make_async_copy(table, table_v, local_sem.at[0]),
        pltpu.make_async_copy(grad, grad_v, local_sem.at[1]),
        pltpu.make_async_copy(counts, counts_v, local_sem.at[2]),
    ]
    fetch_left = pltpu.make_async_copy(left.at[slot], left_v, local_sem.at[3])
    fetch_right = pltpu.make_async_copy(right.at[slot], right_v, local_sem.at[4])

    barrier = pltpu.get_barrier_semaphore()

    @pl.when(relays)
    def _():
        for dy, dz in YZ_STEPS[:-1]:
            peer = {"dp": lax.rem(y + dy, NY) * NXC + xc, "tensor": lax.rem(z + dz, NZ)}
            pl.semaphore_signal(barrier, inc=1, device_id=peer, device_id_type=MESH)

    @pl.when(handles)
    def _():
        for step in range(1, NXC):
            peer = {"dp": y * NXC + lax.rem(xc + step, NXC)}
            pl.semaphore_signal(barrier, inc=1, device_id=peer, device_id_type=MESH)
        fetch_left.start()
        fetch_right.start()

    for copy in fetch:
        copy.start()

    order = reorder(256, lambda k: (k & 128) + ((k & 1) << 6) + (((k >> 4) & 7) << 3) + ((k >> 1) & 7))
    block = iota((NB, NB), 0)
    fetch[0].wait()
    hit = [block == table_v[c : c + 1, :] for c in (0, 1)]
    pick = dot_nt(order, one_where(jnp.concatenate(hit, axis=1))).astype(BF16)
    fetch[1].wait()
    pieces = [dot_nt(pick, grad_v[128 * h : 128 * h + 128, :]).reshape(32, 8, 128) for h in (0, 1)]
    send1[...] = jnp.concatenate(pieces, axis=1).astype(BF16).reshape(PLANES, NY, 16, 128)

    def prepare():
        fetch[2].wait()
        for c in (0, 1):
            live = one_where(hit[c] & (counts_v[0:1, :] > c))
            for h in (0, 1):
                by_owner = reorder(NB, lambda k: ((k & 15) << 4) + (h << 3) + (k >> 4), 256)
                place[c, h] = dot_nt(by_owner, live).astype(BF16)
        ungroup[...] = reorder(256, lambda k: (((k >> 1) & 15) << 4) + ((k & 1) << 3) + (k >> 5))

    pl.when(relays)(prepare)

    @pl.when(handles)
    def _():
        rows = reorder(BLK, lambda k: ((k & 1) << 8) + (k >> 1))
        columns = reorder(BLK, lambda k: (((k >> 1) & 7) << 6) + (((k >> 4) & 15) << 2) + ((k & 1) << 1) + (k >> 8))
        fetch_left.wait()
        high, low = split(left_v[...])
        left_high[...] = dot(dot(rows, high).astype(BF16), columns).astype(BF16)
        left_low[...] = dot(dot(rows, low).astype(BF16), columns).astype(BF16)
        fetch_right.wait()
        high, low = split(right_v[...])
        right_high[...] = high
        right_low[...] = low

    awaited = jnp.where(relays, PLANES * NY - 1 + jnp.where(handles, 7, 8), PLANES * NY)
    pl.semaphore_wait(barrier, awaited)

    def put(source, target, sent_on, lands_on, device):
        pltpu.make_async_remote_copy(
            src_ref=source,
            dst_ref=target,
            send_sem=sent_on,
            recv_sem=lands_on,
            device_id=device,
            device_id_type=MESH,
        ).start()

    def put_unless_here(here, source, target, sent_on, lands_on, device):
        @pl.when(jnp.logical_not(here))
        def _():
            put(source, target, sent_on, lands_on, device)

        @pl.when(here)
        def _():
            pltpu.make_async_copy(source, target, lands_on).start()

    def take(ref, sem):
        pltpu.make_async_copy(ref, ref, sem).wait()

    batch = jnp.where(z < 4, 0, z // 2 - 1)
    for dy in (0, 4, 1, 3, 7, 5, 2, 6):
        there = lax.rem(y + dy, NY)
        for plane in (3, 2, 1, 0):
            source, target = send1.at[plane, there], recv1.at[z, y]
            device = {"dp": there * NXC + xc, "tensor": plane}
            if dy:
                put(source, target, send_sem.at[0], piece_sem.at[batch], device)
            else:
                put_unless_here(z == plane, source, target, send_sem.at[0], piece_sem.at[batch], device)

    pl.when(jnp.logical_not(relays))(prepare)

    @pl.when(relays)
    def _():
        turn = reorder(128, lambda k: ((k & 7) << 4) + ((k >> 4) << 1) + ((k >> 3) & 1))
        for batch, (start, size) in enumerate(BATCHES):
            planes = pl.ds(start, size)
            take(recv1.at[planes], piece_sem.at[batch])
            arrived = [recv1[t].reshape(128, 128) for t in range(start, start + size)]
            turned = dot(turn, jnp.concatenate(arrived, axis=1)).astype(BF16)
            for k in range(size):
                send2[start + k] = turned[:, 128 * k : 128 * k + 128].reshape(NX, 16, 128)
            lands_on = panel_sem.at[start // 4]
            for dx in FAR_FIRST:
                there = lax.rem(x + dx, NX)
                source, target = send2.at[planes, there], recv2.at[planes, xc]
                device = {"dp": y * NXC + there * 2 + lax.rem(z, 2)}
                if dx:
                    put(source, target, send_sem.at[1], lands_on, device)
                else:
                    put_unless_here(handles, source, target, send_sem.at[1], lands_on, device)

    @pl.when(handles)
    def _():
        def half(u):
            take(recv2.at[pl.ds(4 * u, 4)], panel_sem.at[u])
            panels = [recv2[t].reshape(256, 128) for t in range(4 * u, 4 * u + 4)]
            even = jnp.concatenate([panel[:, :64] for panel in panels], axis=1)
            odd = jnp.concatenate([panel[:, 64:] for panel in panels], axis=1)
            held = jnp.concatenate([even, odd], axis=0)
            high, low = split(dot(left_high[...], held) + dot(left_low[...], held))
            first, second = right_high[256 * u : 256 * u + 256, :], right_low[256 * u : 256 * u + 256, :]
            wide = held.astype(F32)
            return dot(high, first) + dot(low, first) + dot(high, second), jnp.sum(wide * wide, keepdims=True)

        partial[...], first_sum = half(0)
        rest, second_sum = half(1)
        direction = partial[...] + rest
        entries = BLK * BLK
        grad_mean = (first_sum + second_sum) / entries
        dir_mean = jnp.sum(direction * direction, keepdims=True) / entries
        factor = jnp.sqrt(grad_mean) * lax.rsqrt(dir_mean + EPSILON)
        mine = (iota((1, NB), 1) == dp) & (counts_v[...] > slot)
        alive = jnp.max(jnp.where(mine, 1.0, 0.0), keepdims=True) > 0.0
        for t in range(0, NZ, 2):
            update = jnp.where(alive, direction[:, 64 * t : 64 * t + 128] * factor, 0.0).astype(BF16)
            upper, lower = update[:256], update[256:]
            first = jnp.concatenate([upper[:, :64], lower[:, :64]], axis=1)
            second = jnp.concatenate([upper[:, 64:], lower[:, 64:]], axis=1)
            send3[:, t] = first.reshape(NY, 32, 128)
            send3[:, t + 1] = second.reshape(NY, 32, 128)
            for plane in (t, t + 1):
                for there in EARLY_Y:
                    source, target = send3.at[there, plane], recv3.at[slot, y]
                    device = {"dp": there * NXC + xc, "tensor": plane}
                    if plane < PLANES:
                        here = (there == y) & (plane == z)
                        put_unless_here(here, source, target, send_sem.at[2], recv_sem.at[slot], device)
                    else:
                        put(source, target, send_sem.at[2], recv_sem.at[slot], device)

    for c in (0, 1):
        take(recv3.at[c], recv_sem.at[c])
        grouped = dot(ungroup[...], recv3[c].reshape(256, 128)).astype(BF16)
        send4[c] = grouped.reshape(NXC, 16, 128)
        for there_x in EARLY_X:
            for there in (there_x * 2 + 1, there_x * 2):
                source, target, lands_on = send4.at[c, there], recv4.at[c, xc], recv_sem.at[2 + c]
                device = {"dp": y * NXC + there}
                put_unless_here(there == xc, source, target, send_sem.at[3], lands_on, device)

    halves = [jnp.zeros((128, NB), F32)] * 2
    for c in (0, 1):
        take(recv4.at[c], recv_sem.at[2 + c])
        returned = recv4[c].reshape(256, 128)
        halves = [halves[h] + dot_tn(returned, place[c, h]) for h in (0, 1)]
    out[...] = jnp.concatenate(halves, axis=0).astype(BF16)

    take(send4.at[:, pl.ds(0, 15)], send_sem.at[3])

    @pl.when(relays)
    def _():
        take(send1.at[pl.ds(0, 3)], send_sem.at[0])
        take(send1.at[3, pl.ds(0, 7)], send_sem.at[0])
        take(send2.at[:, pl.ds(0, 7)], send_sem.at[1])

    @pl.when(jnp.logical_not(relays))
    def _():
        take(send1, send_sem.at[0])

    @pl.when(relays & jnp.logical_not(handles))
    def _():
        take(send2.at[:, 7], send_sem.at[1])

    @pl.when(handles)
    def _():
        take(send3.at[pl.ds(0, 7)], send_sem.at[2])
        take(send3.at[7, pl.ds(0, 7)], send_sem.at[2])


def body(gradient, left_root, right_root, counts, slot_table):
    pieces = jnp.transpose(gradient, (1, 2, 0)).reshape(256, NB)
    operands = (pieces, left_root, right_root, counts.reshape(1, NB), slot_table.T)
    operands = [pltpu.with_memory_space_constraint(operand, pltpu.HBM) for operand in operands]
    vmem = pltpu.VMEM
    message = (32, 128)
    update = pl.pallas_call(
        kernel,
        out_shape=jax.ShapeDtypeStruct((256, NB), BF16),
        in_specs=[pl.BlockSpec(memory_space=pltpu.HBM)] * 5,
        out_specs=pl.BlockSpec(memory_space=pltpu.VMEM),
        scratch_shapes=[
            vmem((256, NB), BF16),
            vmem((BLK, BLK), F32),
            vmem((BLK, BLK), F32),
            vmem((1, NB), jnp.int32),
            vmem((2, NB), jnp.int32),
            vmem((PLANES, NY, 16, 128), BF16),
            vmem((NZ, NY, 16, 128), BF16),
            vmem((NZ, NX, 16, 128), BF16),
            vmem((NZ, NXC, 16, 128), BF16),
            vmem((NY, NZ, *message), BF16),
            vmem((2, NY, *message), BF16),
            vmem((2, NXC, 16, 128), BF16),
            vmem((2, NXC, 16, 128), BF16),
            vmem((BLK, BLK), BF16),
            vmem((BLK, BLK), BF16),
            vmem((BLK, BLK), BF16),
            vmem((BLK, BLK), BF16),
            vmem((256, 256), BF16),
            vmem((2, 2, 256, NB), BF16),
            vmem((BLK, BLK), F32),
            pltpu.SemaphoreType.DMA((5,)),
            pltpu.SemaphoreType.DMA((4,)),
            pltpu.SemaphoreType.DMA((4,)),
            pltpu.SemaphoreType.DMA((3,)),
            pltpu.SemaphoreType.DMA((2,)),
        ],
        compiler_params=pltpu.CompilerParams(
            collective_id=0, has_side_effects=True, vmem_limit_bytes=40 * 1024 * 1024
        ),
    )(*operands)
    return jnp.transpose(update.reshape(4, 64, NB), (2, 0, 1))


def solution(mesh):
    return jax.shard_map(
        body,
        mesh=mesh,
        in_specs=(P(None, "dp", "tensor"), P("dp", None, None), P("dp", None, None), P(), P()),
        out_specs=P(None, "dp", "tensor"),
        check_vma=False,
    )
```

```python
import jax
import jax.numpy as jnp
from jax import lax
from jax.experimental import pallas as pl
from jax.experimental.pallas import tpu as pltpu
from jax.sharding import PartitionSpec as P

MESH = pl.DeviceIdType.MESH
EPSILON = 1e-06
BLK = 512
NB = 128
NY, NX, NXC, NZ = 8, 8, 16, 8
F32, BF16 = jnp.float32, jnp.bfloat16
PLANES = 4
FAR_FIRST = (4, 3, 5, 2, 6, 1, 7, 0)
YZ_STEPS = sorted(((dy, dz) for dy in range(8) for dz in range(8)), key=lambda s: -min(s[0], 8 - s[0]) - min(s[1], 8 - s[1]))
BATCHES = ((0, 4), (4, 2), (6, 2))
EARLY_X = (0, 1, 2, 7, 3, 6, 5, 4)
EARLY_Y = (0, 1, 2, 3, 7, 6, 5, 4)


def iota(shape, dim):
    return lax.broadcasted_iota(jnp.int32, shape, dim)


def one_where(mask):
    return jnp.where(mask, 1.0, 0.0).astype(BF16)


def reorder(n, place_of, rows=None):
    return one_where(iota((rows or n, n), 0) == place_of(iota((1, n), 1)))


def dot(a, b):
    return jnp.dot(a, b, preferred_element_type=F32)


def dot_nt(a, b):
    return lax.dot_general(a, b, (((1,), (1,)), ((), ())), preferred_element_type=F32)


def dot_tn(a, b):
    return lax.dot_general(a, b, (((0,), (0,)), ((), ())), preferred_element_type=F32)


def split(value):
    high = value.astype(BF16)
    return high, (value - high.astype(F32)).astype(BF16)


def kernel(
    grad, left, right, counts, table, out,
    grad_v, left_v, right_v, counts_v, table_v,
    send1, recv1, send2, recv2, send3, recv3, send4, recv4,
    left_high, left_low, right_high, right_low, ungroup, place, partial,
    local_sem, send_sem, recv_sem, piece_sem, panel_sem, late_sem,
):
    dp, z = lax.axis_index("dp"), lax.axis_index("tensor")
    y, xc = dp // NXC, lax.rem(dp, NXC)
    x, core = xc // 2, lax.rem(xc, 2)
    slot = lax.rem(z // 2, 2)
    relays = z < PLANES
    handles = relays & (core == lax.rem(z, 2))

    fetch = [
        pltpu.make_async_copy(table, table_v, local_sem.at[0]),
        pltpu.make_async_copy(grad, grad_v, local_sem.at[1]),
        pltpu.make_async_copy(counts, counts_v, local_sem.at[2]),
    ]
    fetch_left = pltpu.make_async_copy(left.at[slot], left_v, local_sem.at[3])
    fetch_right = pltpu.make_async_copy(right.at[slot], right_v, local_sem.at[4])

    barrier = pltpu.get_barrier_semaphore()

    @pl.when(relays)
    def _():
        for dy, dz in YZ_STEPS[:-1]:
            @pl.when((z < 3) | (dz not in (5, 6, 7)))
            def _(dy=dy, dz=dz):
                peer = {"dp": lax.rem(y + dy, NY) * NXC + xc, "tensor": lax.rem(z + dz, NZ)}
                pl.semaphore_signal(barrier, inc=1, device_id=peer, device_id_type=MESH)

    @pl.when(handles)
    def _():
        for step in range(1, NXC):
            peer = {"dp": y * NXC + lax.rem(xc + step, NXC)}
            pl.semaphore_signal(barrier, inc=1, device_id=peer, device_id_type=MESH)
        fetch_left.start()
        fetch_right.start()

    for copy in fetch:
        copy.start()

    order = reorder(256, lambda k: (k & 128) + ((k & 1) << 6) + (((k >> 4) & 7) << 3) + ((k >> 1) & 7))
    block = iota((NB, NB), 0)
    fetch[0].wait()
    hit = [block == table_v[c : c + 1, :] for c in (0, 1)]
    pick = dot_nt(order, one_where(jnp.concatenate(hit, axis=1))).astype(BF16)
    fetch[1].wait()
    pieces = [dot_nt(pick, grad_v[128 * h : 128 * h + 128, :]).reshape(32, 8, 128) for h in (0, 1)]
    send1[...] = jnp.concatenate(pieces, axis=1).astype(BF16).reshape(PLANES, NY, 16, 128)

    def prepare():
        fetch[2].wait()
        for c in (0, 1):
            live = one_where(hit[c] & (counts_v[0:1, :] > c))
            for h in (0, 1):
                by_owner = reorder(NB, lambda k: ((k & 15) << 4) + (h << 3) + (k >> 4), 256)
                place[c, h] = dot_nt(by_owner, live).astype(BF16)
        ungroup[...] = reorder(256, lambda k: (((k >> 1) & 15) << 4) + ((k & 1) << 3) + (k >> 5))

    pl.when(z < 3)(prepare)

    def prepare_roots():
        rows = reorder(BLK, lambda k: ((k & 1) << 8) + (k >> 1))
        columns = reorder(BLK, lambda k: (((k >> 1) & 7) << 6) + (((k >> 4) & 15) << 2) + ((k & 1) << 1) + (k >> 8))
        fetch_left.wait()
        high, low = split(left_v[...])
        left_high[...] = dot(dot(rows, high).astype(BF16), columns).astype(BF16)
        left_low[...] = dot(dot(rows, low).astype(BF16), columns).astype(BF16)
        fetch_right.wait()
        high, low = split(right_v[...])
        right_high[...] = high
        right_low[...] = low

    pl.when(handles & (z < 3))(prepare_roots)

    awaited = jnp.where(z < 3, 3 * NY, PLANES * NY) + jnp.where(relays, jnp.where(handles, 6, 7), 0)
    pl.semaphore_wait(barrier, awaited)

    @pl.when(z == 3)
    def _():
        for dy in FAR_FIRST:
            for plane in (0, 1, 2):
                peer = {"dp": lax.rem(y + dy, NY) * NXC + xc, "tensor": plane}
                pl.semaphore_signal(late_sem, inc=1, device_id=peer, device_id_type=MESH)

    def put(source, target, sent_on, lands_on, device):
        pltpu.make_async_remote_copy(
            src_ref=source,
            dst_ref=target,
            send_sem=sent_on,
            recv_sem=lands_on,
            device_id=device,
            device_id_type=MESH,
        ).start()

    def put_unless_here(here, source, target, sent_on, lands_on, device):
        @pl.when(jnp.logical_not(here))
        def _():
            put(source, target, sent_on, lands_on, device)

        @pl.when(here)
        def _():
            pltpu.make_async_copy(source, target, lands_on).start()

    def take(ref, sem):
        pltpu.make_async_copy(ref, ref, sem).wait()

    batch = jnp.where(z < 4, 0, z // 2 - 1)
    for plane in (2, 1, 0, 3):
        if plane == 3:

            @pl.when(z < 3)
            def _():
                pl.semaphore_wait(late_sem, NY)

        for dy in FAR_FIRST:
            there = lax.rem(y + dy, NY)
            source, target = send1.at[plane, there], recv1.at[z, y]
            device = {"dp": there * NXC + xc, "tensor": plane}
            if dy:
                put(source, target, send_sem.at[0], piece_sem.at[batch], device)
            else:
                put_unless_here(z == plane, source, target, send_sem.at[0], piece_sem.at[batch], device)

    pl.when(z >= 3)(prepare)
    pl.when(handles & (z >= 3))(prepare_roots)

    @pl.when(relays)
    def _():
        turn = reorder(128, lambda k: ((k & 7) << 4) + ((k >> 4) << 1) + ((k >> 3) & 1))
        for batch, (start, size) in enumerate(BATCHES):
            planes = pl.ds(start, size)
            take(recv1.at[planes], piece_sem.at[batch])
            arrived = [recv1[t].reshape(128, 128) for t in range(start, start + size)]
            turned = dot(turn, jnp.concatenate(arrived, axis=1)).astype(BF16)
            for k in range(size):
                send2[start + k] = turned[:, 128 * k : 128 * k + 128].reshape(NX, 16, 128)
            lands_on = panel_sem.at[start // 4]
            for dx in FAR_FIRST:
                there = lax.rem(x + dx, NX)
                source, target = send2.at[planes, there], recv2.at[planes, xc]
                device = {"dp": y * NXC + there * 2 + lax.rem(z, 2)}
                if dx:
                    put(source, target, send_sem.at[1], lands_on, device)
                else:
                    put_unless_here(handles, source, target, send_sem.at[1], lands_on, device)

    @pl.when(handles)
    def _():
        def half(u):
            take(recv2.at[pl.ds(4 * u, 4)], panel_sem.at[u])
            panels = [recv2[t].reshape(256, 128) for t in range(4 * u, 4 * u + 4)]
            even = jnp.concatenate([panel[:, :64] for panel in panels], axis=1)
            odd = jnp.concatenate([panel[:, 64:] for panel in panels], axis=1)
            held = jnp.concatenate([even, odd], axis=0)
            high, low = split(dot(left_high[...], held) + dot(left_low[...], held))
            first, second = right_high[256 * u : 256 * u + 256, :], right_low[256 * u : 256 * u + 256, :]
            wide = held.astype(F32)
            return dot(high, first) + dot(low, first) + dot(high, second), jnp.sum(wide * wide, keepdims=True)

        partial[...], first_sum = half(0)
        rest, second_sum = half(1)
        direction = partial[...] + rest
        entries = BLK * BLK
        grad_mean = (first_sum + second_sum) / entries
        dir_mean = jnp.sum(direction * direction, keepdims=True) / entries
        factor = jnp.sqrt(grad_mean) * lax.rsqrt(dir_mean + EPSILON)
        mine = (iota((1, NB), 1) == dp) & (counts_v[...] > slot)
        alive = jnp.max(jnp.where(mine, 1.0, 0.0), keepdims=True) > 0.0
        for t in range(0, NZ, 2):
            update = jnp.where(alive, direction[:, 64 * t : 64 * t + 128] * factor, 0.0).astype(BF16)
            upper, lower = update[:256], update[256:]
            first = jnp.concatenate([upper[:, :64], lower[:, :64]], axis=1)
            second = jnp.concatenate([upper[:, 64:], lower[:, 64:]], axis=1)
            send3[:, t] = first.reshape(NY, 32, 128)
            send3[:, t + 1] = second.reshape(NY, 32, 128)
            for plane in (t, t + 1):
                for there in EARLY_Y:
                    source, target = send3.at[there, plane], recv3.at[slot, y]
                    device = {"dp": there * NXC + xc, "tensor": plane}
                    if plane < PLANES:
                        here = (there == y) & (plane == z)
                        put_unless_here(here, source, target, send_sem.at[2], recv_sem.at[slot], device)
                    else:
                        put(source, target, send_sem.at[2], recv_sem.at[slot], device)

    for c in (0, 1):
        take(recv3.at[c], recv_sem.at[c])
        grouped = dot(ungroup[...], recv3[c].reshape(256, 128)).astype(BF16)
        send4[c] = grouped.reshape(NXC, 16, 128)
        for there_x in EARLY_X:
            for there in (there_x * 2 + 1, there_x * 2):
                source, target, lands_on = send4.at[c, there], recv4.at[c, xc], recv_sem.at[2 + c]
                device = {"dp": y * NXC + there}
                put_unless_here(there == xc, source, target, send_sem.at[3], lands_on, device)

    halves = [jnp.zeros((128, NB), F32)] * 2
    for c in (0, 1):
        take(recv4.at[c], recv_sem.at[2 + c])
        returned = recv4[c].reshape(256, 128)
        halves = [halves[h] + dot_tn(returned, place[c, h]) for h in (0, 1)]
    out[...] = jnp.concatenate(halves, axis=0).astype(BF16)

    take(send4.at[:, pl.ds(0, 15)], send_sem.at[3])

    @pl.when(relays)
    def _():
        take(send1.at[pl.ds(0, 3)], send_sem.at[0])
        take(send1.at[3, pl.ds(0, 7)], send_sem.at[0])
        take(send2.at[:, pl.ds(0, 7)], send_sem.at[1])

    @pl.when(jnp.logical_not(relays))
    def _():
        take(send1, send_sem.at[0])

    @pl.when(relays & jnp.logical_not(handles))
    def _():
        take(send2.at[:, 7], send_sem.at[1])

    @pl.when(handles)
    def _():
        take(send3.at[pl.ds(0, 7)], send_sem.at[2])
        take(send3.at[7, pl.ds(0, 7)], send_sem.at[2])


def body(gradient, left_root, right_root, counts, slot_table):
    pieces = jnp.transpose(gradient, (1, 2, 0)).reshape(256, NB)
    operands = (pieces, left_root, right_root, counts.reshape(1, NB), slot_table.T)
    operands = [pltpu.with_memory_space_constraint(operand, pltpu.HBM) for operand in operands]
    vmem = pltpu.VMEM
    message = (32, 128)
    update = pl.pallas_call(
        kernel,
        out_shape=jax.ShapeDtypeStruct((256, NB), BF16),
        in_specs=[pl.BlockSpec(memory_space=pltpu.HBM)] * 5,
        out_specs=pl.BlockSpec(memory_space=pltpu.VMEM),
        scratch_shapes=[
            vmem((256, NB), BF16),
            vmem((BLK, BLK), F32),
            vmem((BLK, BLK), F32),
            vmem((1, NB), jnp.int32),
            vmem((2, NB), jnp.int32),
            vmem((PLANES, NY, 16, 128), BF16),
            vmem((NZ, NY, 16, 128), BF16),
            vmem((NZ, NX, 16, 128), BF16),
            vmem((NZ, NXC, 16, 128), BF16),
            vmem((NY, NZ, *message), BF16),
            vmem((2, NY, *message), BF16),
            vmem((2, NXC, 16, 128), BF16),
            vmem((2, NXC, 16, 128), BF16),
            vmem((BLK, BLK), BF16),
            vmem((BLK, BLK), BF16),
            vmem((BLK, BLK), BF16),
            vmem((BLK, BLK), BF16),
            vmem((256, 256), BF16),
            vmem((2, 2, 256, NB), BF16),
            vmem((BLK, BLK), F32),
            pltpu.SemaphoreType.DMA((5,)),
            pltpu.SemaphoreType.DMA((4,)),
            pltpu.SemaphoreType.DMA((4,)),
            pltpu.SemaphoreType.DMA((3,)),
            pltpu.SemaphoreType.DMA((2,)),
            pltpu.SemaphoreType.REGULAR,
        ],
        compiler_params=pltpu.CompilerParams(
            collective_id=0, has_side_effects=True, vmem_limit_bytes=40 * 1024 * 1024
        ),
    )(*operands)
    return jnp.transpose(update.reshape(4, 64, NB), (2, 0, 1))


def solution(mesh):
    return jax.shard_map(
        body,
        mesh=mesh,
        in_specs=(P(None, "dp", "tensor"), P("dp", None, None), P("dp", None, None), P(), P()),
        out_specs=P(None, "dp", "tensor"),
        check_vma=False,
    )
```

```python
import jax
import jax.numpy as jnp
from jax import lax
from jax.experimental import pallas as pl
from jax.experimental.pallas import tpu as pltpu
from jax.sharding import PartitionSpec as P

MESH = pl.DeviceIdType.MESH
EPSILON = 1e-06
BLK = 512
NB = 128
NY, NX, NXC, NZ = 8, 8, 16, 8
F32, BF16 = jnp.float32, jnp.bfloat16
PLANES = 4
FAR_FIRST = (4, 3, 5, 2, 6, 1, 7, 0)
YZ_STEPS = sorted(((dy, dz) for dy in range(8) for dz in range(8)), key=lambda s: -min(s[0], 8 - s[0]) - min(s[1], 8 - s[1]))
BATCHES = ((0, 4), (4, 2), (6, 2))
EARLY_X = (0, 1, 2, 7, 3, 6, 5, 4)
EARLY_Y = (0, 1, 2, 3, 7, 6, 5, 4)


def iota(shape, dim):
    return lax.broadcasted_iota(jnp.int32, shape, dim)


def one_where(mask):
    return jnp.where(mask, 1.0, 0.0).astype(BF16)


def reorder(n, place_of, rows=None):
    return one_where(iota((rows or n, n), 0) == place_of(iota((1, n), 1)))


def dot(a, b):
    return jnp.dot(a, b, preferred_element_type=F32)


def dot_nt(a, b):
    return lax.dot_general(a, b, (((1,), (1,)), ((), ())), preferred_element_type=F32)


def dot_tn(a, b):
    return lax.dot_general(a, b, (((0,), (0,)), ((), ())), preferred_element_type=F32)


def split(value):
    high = value.astype(BF16)
    return high, (value - high.astype(F32)).astype(BF16)


def kernel(
    grad, left, right, counts, table, out,
    grad_v, left_v, right_v, counts_v, table_v,
    send1, recv1, send2, recv2, send3, recv3, send4, recv4,
    left_high, left_low, right_high, right_low, ungroup, place, partial,
    local_sem, send_sem, recv_sem, piece_sem, panel_sem,
):
    dp, z = lax.axis_index("dp"), lax.axis_index("tensor")
    y, xc = dp // NXC, lax.rem(dp, NXC)
    x, core = xc // 2, lax.rem(xc, 2)
    slot = lax.rem(z // 2, 2)
    relays = z < PLANES
    handles = relays & (core == lax.rem(z, 2))

    fetch = [
        pltpu.make_async_copy(table, table_v, local_sem.at[0]),
        pltpu.make_async_copy(grad, grad_v, local_sem.at[1]),
        pltpu.make_async_copy(counts, counts_v, local_sem.at[2]),
    ]
    fetch_left = pltpu.make_async_copy(left.at[slot], left_v, local_sem.at[3])
    fetch_right = pltpu.make_async_copy(right.at[slot], right_v, local_sem.at[4])

    barrier = pltpu.get_barrier_semaphore()

    @pl.when(relays)
    def _():
        for dy, dz in YZ_STEPS[:-1]:
            peer = {"dp": lax.rem(y + dy, NY) * NXC + xc, "tensor": lax.rem(z + dz, NZ)}
            pl.semaphore_signal(barrier, inc=1, device_id=peer, device_id_type=MESH)

    @pl.when(handles)
    def _():
        for step in range(1, NXC):
            peer = {"dp": y * NXC + lax.rem(xc + step, NXC)}
            pl.semaphore_signal(barrier, inc=1, device_id=peer, device_id_type=MESH)
        fetch_left.start()
        fetch_right.start()

    for copy in fetch:
        copy.start()

    order = reorder(256, lambda k: (k & 128) + ((k & 1) << 6) + (((k >> 4) & 7) << 3) + ((k >> 1) & 7))
    block = iota((NB, NB), 0)
    fetch[0].wait()
    hit = [block == table_v[c : c + 1, :] for c in (0, 1)]
    pick = dot_nt(order, one_where(jnp.concatenate(hit, axis=1))).astype(BF16)
    fetch[1].wait()

    def prepare():
        fetch[2].wait()
        for c in (0, 1):
            live = one_where(hit[c] & (counts_v[0:1, :] > c))
            for h in (0, 1):
                by_owner = reorder(NB, lambda k: ((k & 15) << 4) + (h << 3) + (k >> 4), 256)
                place[c, h] = dot_nt(by_owner, live).astype(BF16)
        ungroup[...] = reorder(256, lambda k: (((k >> 1) & 15) << 4) + ((k & 1) << 3) + (k >> 5))

    pl.when(relays)(prepare)

    @pl.when(handles)
    def _():
        rows = reorder(BLK, lambda k: ((k & 1) << 8) + (k >> 1))
        columns = reorder(BLK, lambda k: (((k >> 1) & 7) << 6) + (((k >> 4) & 15) << 2) + ((k & 1) << 1) + (k >> 8))
        fetch_left.wait()
        high, low = split(left_v[...])
        left_high[...] = dot(dot(rows, high).astype(BF16), columns).astype(BF16)
        left_low[...] = dot(dot(rows, low).astype(BF16), columns).astype(BF16)
        fetch_right.wait()
        high, low = split(right_v[...])
        right_high[...] = high
        right_low[...] = low

    awaited = jnp.where(relays, PLANES * NY - 1 + jnp.where(handles, 7, 8), PLANES * NY)
    pl.semaphore_wait(barrier, awaited)

    def put(source, target, sent_on, lands_on, device):
        pltpu.make_async_remote_copy(
            src_ref=source,
            dst_ref=target,
            send_sem=sent_on,
            recv_sem=lands_on,
            device_id=device,
            device_id_type=MESH,
        ).start()

    def put_unless_here(here, source, target, sent_on, lands_on, device):
        @pl.when(jnp.logical_not(here))
        def _():
            put(source, target, sent_on, lands_on, device)

        @pl.when(here)
        def _():
            pltpu.make_async_copy(source, target, lands_on).start()

    def take(ref, sem):
        pltpu.make_async_copy(ref, ref, sem).wait()

    batch = jnp.where(z < 4, 0, z // 2 - 1)
    for plane in (3, 2, 1, 0):
        chosen = pick[64 * plane : 64 * plane + 64]
        pieces = [dot_nt(chosen, grad_v[128 * h : 128 * h + 128, :]).reshape(NY, 8, 128) for h in (0, 1)]
        send1[plane] = jnp.concatenate(pieces, axis=1).astype(BF16)
        for dy in (0, 4, 1, 3, 7, 5, 2, 6):
            there = lax.rem(y + dy, NY)
            source, target = send1.at[plane, there], recv1.at[z, y]
            device = {"dp": there * NXC + xc, "tensor": plane}
            if dy:
                put(source, target, send_sem.at[0], piece_sem.at[batch], device)
            else:
                put_unless_here(z == plane, source, target, send_sem.at[0], piece_sem.at[batch], device)

    pl.when(jnp.logical_not(relays))(prepare)

    @pl.when(relays)
    def _():
        turn = reorder(128, lambda k: ((k & 7) << 4) + ((k >> 4) << 1) + ((k >> 3) & 1))
        for batch, (start, size) in enumerate(BATCHES):
            planes = pl.ds(start, size)
            take(recv1.at[planes], piece_sem.at[batch])
            arrived = [recv1[t].reshape(128, 128) for t in range(start, start + size)]
            turned = dot(turn, jnp.concatenate(arrived, axis=1)).astype(BF16)
            for k in range(size):
                send2[start + k] = turned[:, 128 * k : 128 * k + 128].reshape(NX, 16, 128)
            lands_on = panel_sem.at[start // 4]
            for dx in FAR_FIRST:
                there = lax.rem(x + dx, NX)
                source, target = send2.at[planes, there], recv2.at[planes, xc]
                device = {"dp": y * NXC + there * 2 + lax.rem(z, 2)}
                if dx:
                    put(source, target, send_sem.at[1], lands_on, device)
                else:
                    put_unless_here(handles, source, target, send_sem.at[1], lands_on, device)

    @pl.when(handles)
    def _():
        def half(u):
            take(recv2.at[pl.ds(4 * u, 4)], panel_sem.at[u])
            panels = [recv2[t].reshape(256, 128) for t in range(4 * u, 4 * u + 4)]
            even = jnp.concatenate([panel[:, :64] for panel in panels], axis=1)
            odd = jnp.concatenate([panel[:, 64:] for panel in panels], axis=1)
            held = jnp.concatenate([even, odd], axis=0)
            high, low = split(dot(left_high[...], held) + dot(left_low[...], held))
            first, second = right_high[256 * u : 256 * u + 256, :], right_low[256 * u : 256 * u + 256, :]
            wide = held.astype(F32)
            return dot(high, first) + dot(low, first) + dot(high, second), jnp.sum(wide * wide, keepdims=True)

        partial[...], first_sum = half(0)
        rest, second_sum = half(1)
        direction = partial[...] + rest
        entries = BLK * BLK
        grad_mean = (first_sum + second_sum) / entries
        dir_mean = jnp.sum(direction * direction, keepdims=True) / entries
        factor = jnp.sqrt(grad_mean) * lax.rsqrt(dir_mean + EPSILON)
        mine = (iota((1, NB), 1) == dp) & (counts_v[...] > slot)
        alive = jnp.max(jnp.where(mine, 1.0, 0.0), keepdims=True) > 0.0
        for t in range(0, NZ, 2):
            update = jnp.where(alive, direction[:, 64 * t : 64 * t + 128] * factor, 0.0).astype(BF16)
            upper, lower = update[:256], update[256:]
            first = jnp.concatenate([upper[:, :64], lower[:, :64]], axis=1)
            second = jnp.concatenate([upper[:, 64:], lower[:, 64:]], axis=1)
            send3[:, t] = first.reshape(NY, 32, 128)
            send3[:, t + 1] = second.reshape(NY, 32, 128)
            for plane in (t, t + 1):
                for there in EARLY_Y:
                    source, target = send3.at[there, plane], recv3.at[slot, y]
                    device = {"dp": there * NXC + xc, "tensor": plane}
                    if plane < PLANES:
                        here = (there == y) & (plane == z)
                        put_unless_here(here, source, target, send_sem.at[2], recv_sem.at[slot], device)
                    else:
                        put(source, target, send_sem.at[2], recv_sem.at[slot], device)

    for c in (0, 1):
        take(recv3.at[c], recv_sem.at[c])
        grouped = dot(ungroup[...], recv3[c].reshape(256, 128)).astype(BF16)
        send4[c] = grouped.reshape(NXC, 16, 128)
        for there_x in EARLY_X:
            for there in (there_x * 2 + 1, there_x * 2):
                source, target, lands_on = send4.at[c, there], recv4.at[c, xc], recv_sem.at[2 + c]
                device = {"dp": y * NXC + there}
                put_unless_here(there == xc, source, target, send_sem.at[3], lands_on, device)

    halves = [jnp.zeros((128, NB), F32)] * 2
    for c in (0, 1):
        take(recv4.at[c], recv_sem.at[2 + c])
        returned = recv4[c].reshape(256, 128)
        halves = [halves[h] + dot_tn(returned, place[c, h]) for h in (0, 1)]
    out[...] = jnp.concatenate(halves, axis=0).astype(BF16)

    take(send4.at[:, pl.ds(0, 15)], send_sem.at[3])

    @pl.when(relays)
    def _():
        take(send1.at[pl.ds(0, 3)], send_sem.at[0])
        take(send1.at[3, pl.ds(0, 7)], send_sem.at[0])
        take(send2.at[:, pl.ds(0, 7)], send_sem.at[1])

    @pl.when(jnp.logical_not(relays))
    def _():
        take(send1, send_sem.at[0])

    @pl.when(relays & jnp.logical_not(handles))
    def _():
        take(send2.at[:, 7], send_sem.at[1])

    @pl.when(handles)
    def _():
        take(send3.at[pl.ds(0, 7)], send_sem.at[2])
        take(send3.at[7, pl.ds(0, 7)], send_sem.at[2])


def body(gradient, left_root, right_root, counts, slot_table):
    pieces = jnp.transpose(gradient, (1, 2, 0)).reshape(256, NB)
    operands = (pieces, left_root, right_root, counts.reshape(1, NB), slot_table.T)
    operands = [pltpu.with_memory_space_constraint(operand, pltpu.HBM) for operand in operands]
    vmem = pltpu.VMEM
    message = (32, 128)
    update = pl.pallas_call(
        kernel,
        out_shape=jax.ShapeDtypeStruct((256, NB), BF16),
        in_specs=[pl.BlockSpec(memory_space=pltpu.HBM)] * 5,
        out_specs=pl.BlockSpec(memory_space=pltpu.VMEM),
        scratch_shapes=[
            vmem((256, NB), BF16),
            vmem((BLK, BLK), F32),
            vmem((BLK, BLK), F32),
            vmem((1, NB), jnp.int32),
            vmem((2, NB), jnp.int32),
            vmem((PLANES, NY, 16, 128), BF16),
            vmem((NZ, NY, 16, 128), BF16),
            vmem((NZ, NX, 16, 128), BF16),
            vmem((NZ, NXC, 16, 128), BF16),
            vmem((NY, NZ, *message), BF16),
            vmem((2, NY, *message), BF16),
            vmem((2, NXC, 16, 128), BF16),
            vmem((2, NXC, 16, 128), BF16),
            vmem((BLK, BLK), BF16),
            vmem((BLK, BLK), BF16),
            vmem((BLK, BLK), BF16),
            vmem((BLK, BLK), BF16),
            vmem((256, 256), BF16),
            vmem((2, 2, 256, NB), BF16),
            vmem((BLK, BLK), F32),
            pltpu.SemaphoreType.DMA((5,)),
            pltpu.SemaphoreType.DMA((4,)),
            pltpu.SemaphoreType.DMA((4,)),
            pltpu.SemaphoreType.DMA((3,)),
            pltpu.SemaphoreType.DMA((2,)),
        ],
        compiler_params=pltpu.CompilerParams(
            collective_id=0, has_side_effects=True, vmem_limit_bytes=40 * 1024 * 1024
        ),
    )(*operands)
    return jnp.transpose(update.reshape(4, 64, NB), (2, 0, 1))


def solution(mesh):
    return jax.shard_map(
        body,
        mesh=mesh,
        in_specs=(P(None, "dp", "tensor"), P("dp", None, None), P("dp", None, None), P(), P()),
        out_specs=P(None, "dp", "tensor"),
        check_vma=False,
    )
```

```python
import jax
import jax.numpy as jnp
from jax import lax
from jax.experimental import pallas as pl
from jax.experimental.pallas import tpu as pltpu
from jax.sharding import PartitionSpec as P

MESH = pl.DeviceIdType.MESH
EPSILON = 1e-06
BLK = 512
NB = 128
NY, NX, NXC, NZ = 8, 8, 16, 8
F32, BF16 = jnp.float32, jnp.bfloat16
PLANES = 4
FAR_FIRST = (4, 3, 5, 2, 6, 1, 7, 0)
YZ_STEPS = sorted(((dy, dz) for dy in range(8) for dz in range(8)), key=lambda s: -min(s[0], 8 - s[0]) - min(s[1], 8 - s[1]))
BATCHES = ((0, 4), (4, 2), (6, 2))
EARLY_X = (0, 1, 2, 7, 3, 6, 5, 4)
EARLY_Y = (0, 1, 2, 3, 7, 6, 5, 4)


def iota(shape, dim):
    return lax.broadcasted_iota(jnp.int32, shape, dim)


def one_where(mask):
    return jnp.where(mask, 1.0, 0.0).astype(BF16)


def reorder(n, place_of, rows=None):
    return one_where(iota((rows or n, n), 0) == place_of(iota((1, n), 1)))


def dot(a, b):
    return jnp.dot(a, b, preferred_element_type=F32)


def dot_nt(a, b):
    return lax.dot_general(a, b, (((1,), (1,)), ((), ())), preferred_element_type=F32)


def dot_tn(a, b):
    return lax.dot_general(a, b, (((0,), (0,)), ((), ())), preferred_element_type=F32)


def split(value):
    high = value.astype(BF16)
    return high, (value - high.astype(F32)).astype(BF16)


def kernel(
    grad, left, right, counts, table, out,
    grad_v, left_v, right_v, counts_v, table_v,
    send1, recv1, send2, recv2, send3, recv3, send4, recv4,
    left_high, left_low, right_high, right_low, ungroup, place, partial,
    local_sem, send_sem, recv_sem, piece_sem, panel_sem,
):
    dp, z = lax.axis_index("dp"), lax.axis_index("tensor")
    y, xc = dp // NXC, lax.rem(dp, NXC)
    x, core = xc // 2, lax.rem(xc, 2)
    slot = lax.rem(z // 2, 2)
    relays = z < PLANES
    handles = relays & (core == lax.rem(z, 2))

    fetch = [
        pltpu.make_async_copy(table, table_v, local_sem.at[0]),
        pltpu.make_async_copy(grad, grad_v, local_sem.at[1]),
        pltpu.make_async_copy(counts, counts_v, local_sem.at[2]),
    ]
    fetch_left = pltpu.make_async_copy(left.at[slot], left_v, local_sem.at[3])
    fetch_right = pltpu.make_async_copy(right.at[slot], right_v, local_sem.at[4])

    barrier = pltpu.get_barrier_semaphore()

    @pl.when(relays)
    def _():
        for dy, dz in YZ_STEPS[:-1]:
            peer = {"dp": lax.rem(y + dy, NY) * NXC + xc, "tensor": lax.rem(z + dz, NZ)}
            pl.semaphore_signal(barrier, inc=1, device_id=peer, device_id_type=MESH)

    @pl.when(handles)
    def _():
        for step in range(1, NXC):
            peer = {"dp": y * NXC + lax.rem(xc + step, NXC)}
            pl.semaphore_signal(barrier, inc=1, device_id=peer, device_id_type=MESH)
        fetch_left.start()
        fetch_right.start()

    for copy in fetch:
        copy.start()

    order = reorder(256, lambda k: (k & 128) + ((k & 1) << 6) + (((k >> 4) & 7) << 3) + ((k >> 1) & 7))
    block = iota((NB, NB), 0)
    fetch[0].wait()
    hit = [block == table_v[c : c + 1, :] for c in (0, 1)]
    hits = one_where(jnp.concatenate(hit, axis=1))
    fetch[1].wait()

    def prepare():
        fetch[2].wait()
        for c in (0, 1):
            live = one_where(hit[c] & (counts_v[0:1, :] > c))
            for h in (0, 1):
                by_owner = reorder(NB, lambda k: ((k & 15) << 4) + (h << 3) + (k >> 4), 256)
                place[c, h] = dot_nt(by_owner, live).astype(BF16)
        ungroup[...] = reorder(256, lambda k: (((k >> 1) & 15) << 4) + ((k & 1) << 3) + (k >> 5))

    pl.when(relays)(prepare)

    @pl.when(handles)
    def _():
        rows = reorder(BLK, lambda k: ((k & 1) << 8) + (k >> 1))
        columns = reorder(BLK, lambda k: (((k >> 1) & 7) << 6) + (((k >> 4) & 15) << 2) + ((k & 1) << 1) + (k >> 8))
        fetch_left.wait()
        high, low = split(left_v[...])
        left_high[...] = dot(dot(rows, high).astype(BF16), columns).astype(BF16)
        left_low[...] = dot(dot(rows, low).astype(BF16), columns).astype(BF16)
        fetch_right.wait()
        high, low = split(right_v[...])
        right_high[...] = high
        right_low[...] = low

    awaited = jnp.where(relays, PLANES * NY - 1 + jnp.where(handles, 7, 8), PLANES * NY)
    pl.semaphore_wait(barrier, awaited)

    def put(source, target, sent_on, lands_on, device):
        pltpu.make_async_remote_copy(
            src_ref=source,
            dst_ref=target,
            send_sem=sent_on,
            recv_sem=lands_on,
            device_id=device,
            device_id_type=MESH,
        ).start()

    def put_unless_here(here, source, target, sent_on, lands_on, device):
        @pl.when(jnp.logical_not(here))
        def _():
            put(source, target, sent_on, lands_on, device)

        @pl.when(here)
        def _():
            pltpu.make_async_copy(source, target, lands_on).start()

    def take(ref, sem):
        pltpu.make_async_copy(ref, ref, sem).wait()

    batch = jnp.where(z < 4, 0, z // 2 - 1)
    for plane in (3, 2, 1, 0):
        chosen = dot_nt(order[64 * plane : 64 * plane + 64], hits).astype(BF16)
        pieces = [dot_nt(chosen, grad_v[128 * h : 128 * h + 128, :]).reshape(NY, 8, 128) for h in (0, 1)]
        send1[plane] = jnp.concatenate(pieces, axis=1).astype(BF16)
        for dy in (0, 4, 1, 3, 7, 5, 2, 6):
            there = lax.rem(y + dy, NY)
            source, target = send1.at[plane, there], recv1.at[z, y]
            device = {"dp": there * NXC + xc, "tensor": plane}
            if dy:
                put(source, target, send_sem.at[0], piece_sem.at[batch], device)
            else:
                put_unless_here(z == plane, source, target, send_sem.at[0], piece_sem.at[batch], device)

    pl.when(jnp.logical_not(relays))(prepare)

    @pl.when(relays)
    def _():
        turn = reorder(128, lambda k: ((k & 7) << 4) + ((k >> 4) << 1) + ((k >> 3) & 1))
        for batch, (start, size) in enumerate(BATCHES):
            planes = pl.ds(start, size)
            take(recv1.at[planes], piece_sem.at[batch])
            arrived = [recv1[t].reshape(128, 128) for t in range(start, start + size)]
            turned = dot(turn, jnp.concatenate(arrived, axis=1)).astype(BF16)
            for k in range(size):
                send2[start + k] = turned[:, 128 * k : 128 * k + 128].reshape(NX, 16, 128)
            lands_on = panel_sem.at[start // 4]
            for dx in FAR_FIRST:
                there = lax.rem(x + dx, NX)
                source, target = send2.at[planes, there], recv2.at[planes, xc]
                device = {"dp": y * NXC + there * 2 + lax.rem(z, 2)}
                if dx:
                    put(source, target, send_sem.at[1], lands_on, device)
                else:
                    put_unless_here(handles, source, target, send_sem.at[1], lands_on, device)

    @pl.when(handles)
    def _():
        def half(u):
            take(recv2.at[pl.ds(4 * u, 4)], panel_sem.at[u])
            panels = [recv2[t].reshape(256, 128) for t in range(4 * u, 4 * u + 4)]
            even = jnp.concatenate([panel[:, :64] for panel in panels], axis=1)
            odd = jnp.concatenate([panel[:, 64:] for panel in panels], axis=1)
            held = jnp.concatenate([even, odd], axis=0)
            high, low = split(dot(left_high[...], held) + dot(left_low[...], held))
            first, second = right_high[256 * u : 256 * u + 256, :], right_low[256 * u : 256 * u + 256, :]
            wide = held.astype(F32)
            return dot(high, first) + dot(low, first) + dot(high, second), jnp.sum(wide * wide, keepdims=True)

        partial[...], first_sum = half(0)
        rest, second_sum = half(1)
        direction = partial[...] + rest
        entries = BLK * BLK
        grad_mean = (first_sum + second_sum) / entries
        dir_mean = jnp.sum(direction * direction, keepdims=True) / entries
        factor = jnp.sqrt(grad_mean) * lax.rsqrt(dir_mean + EPSILON)
        mine = (iota((1, NB), 1) == dp) & (counts_v[...] > slot)
        alive = jnp.max(jnp.where(mine, 1.0, 0.0), keepdims=True) > 0.0
        for t in range(0, NZ, 2):
            update = jnp.where(alive, direction[:, 64 * t : 64 * t + 128] * factor, 0.0).astype(BF16)
            upper, lower = update[:256], update[256:]
            first = jnp.concatenate([upper[:, :64], lower[:, :64]], axis=1)
            second = jnp.concatenate([upper[:, 64:], lower[:, 64:]], axis=1)
            send3[:, t] = first.reshape(NY, 32, 128)
            send3[:, t + 1] = second.reshape(NY, 32, 128)
            for plane in (t, t + 1):
                for there in EARLY_Y:
                    source, target = send3.at[there, plane], recv3.at[slot, y]
                    device = {"dp": there * NXC + xc, "tensor": plane}
                    if plane < PLANES:
                        here = (there == y) & (plane == z)
                        put_unless_here(here, source, target, send_sem.at[2], recv_sem.at[slot], device)
                    else:
                        put(source, target, send_sem.at[2], recv_sem.at[slot], device)

    for c in (0, 1):
        take(recv3.at[c], recv_sem.at[c])
        grouped = dot(ungroup[...], recv3[c].reshape(256, 128)).astype(BF16)
        send4[c] = grouped.reshape(NXC, 16, 128)
        for there_x in EARLY_X:
            for there in (there_x * 2 + 1, there_x * 2):
                source, target, lands_on = send4.at[c, there], recv4.at[c, xc], recv_sem.at[2 + c]
                device = {"dp": y * NXC + there}
                put_unless_here(there == xc, source, target, send_sem.at[3], lands_on, device)

    halves = [jnp.zeros((128, NB), F32)] * 2
    for c in (0, 1):
        take(recv4.at[c], recv_sem.at[2 + c])
        returned = recv4[c].reshape(256, 128)
        halves = [halves[h] + dot_tn(returned, place[c, h]) for h in (0, 1)]
    out[...] = jnp.concatenate(halves, axis=0).astype(BF16)

    take(send4.at[:, pl.ds(0, 15)], send_sem.at[3])

    @pl.when(relays)
    def _():
        take(send1.at[pl.ds(0, 3)], send_sem.at[0])
        take(send1.at[3, pl.ds(0, 7)], send_sem.at[0])
        take(send2.at[:, pl.ds(0, 7)], send_sem.at[1])

    @pl.when(jnp.logical_not(relays))
    def _():
        take(send1, send_sem.at[0])

    @pl.when(relays & jnp.logical_not(handles))
    def _():
        take(send2.at[:, 7], send_sem.at[1])

    @pl.when(handles)
    def _():
        take(send3.at[pl.ds(0, 7)], send_sem.at[2])
        take(send3.at[7, pl.ds(0, 7)], send_sem.at[2])


def body(gradient, left_root, right_root, counts, slot_table):
    pieces = jnp.transpose(gradient, (1, 2, 0)).reshape(256, NB)
    operands = (pieces, left_root, right_root, counts.reshape(1, NB), slot_table.T)
    operands = [pltpu.with_memory_space_constraint(operand, pltpu.HBM) for operand in operands]
    vmem = pltpu.VMEM
    message = (32, 128)
    update = pl.pallas_call(
        kernel,
        out_shape=jax.ShapeDtypeStruct((256, NB), BF16),
        in_specs=[pl.BlockSpec(memory_space=pltpu.HBM)] * 5,
        out_specs=pl.BlockSpec(memory_space=pltpu.VMEM),
        scratch_shapes=[
            vmem((256, NB), BF16),
            vmem((BLK, BLK), F32),
            vmem((BLK, BLK), F32),
            vmem((1, NB), jnp.int32),
            vmem((2, NB), jnp.int32),
            vmem((PLANES, NY, 16, 128), BF16),
            vmem((NZ, NY, 16, 128), BF16),
            vmem((NZ, NX, 16, 128), BF16),
            vmem((NZ, NXC, 16, 128), BF16),
            vmem((NY, NZ, *message), BF16),
            vmem((2, NY, *message), BF16),
            vmem((2, NXC, 16, 128), BF16),
            vmem((2, NXC, 16, 128), BF16),
            vmem((BLK, BLK), BF16),
            vmem((BLK, BLK), BF16),
            vmem((BLK, BLK), BF16),
            vmem((BLK, BLK), BF16),
            vmem((256, 256), BF16),
            vmem((2, 2, 256, NB), BF16),
            vmem((BLK, BLK), F32),
            pltpu.SemaphoreType.DMA((5,)),
            pltpu.SemaphoreType.DMA((4,)),
            pltpu.SemaphoreType.DMA((4,)),
            pltpu.SemaphoreType.DMA((3,)),
            pltpu.SemaphoreType.DMA((2,)),
        ],
        compiler_params=pltpu.CompilerParams(
            collective_id=0, has_side_effects=True, vmem_limit_bytes=40 * 1024 * 1024
        ),
    )(*operands)
    return jnp.transpose(update.reshape(4, 64, NB), (2, 0, 1))


def solution(mesh):
    return jax.shard_map(
        body,
        mesh=mesh,
        in_specs=(P(None, "dp", "tensor"), P("dp", None, None), P("dp", None, None), P(), P()),
        out_specs=P(None, "dp", "tensor"),
        check_vma=False,
    )
```
